256 devices in a mesh: ctx: 32 (over z, x), head: 8 (over y, core).
Axes of the slice: x: 4, y: 4, z: 8, core: 2. Of those that a mesh axis runs over, the one named last changes fastest.
Arguments:
- state_query: bfloat16 [16384, 4096], P('ctx', 'head'), may hold values from -6 to 6
- state_key: bfloat16 [16384, 4096], P('ctx', 'head'), may hold values from -0.5 to 0.5
- state_value: bfloat16 [16384, 4096], P('ctx', 'head'), may hold values from -6 to 6
- state_gate: bfloat16 [16384, 4096], P('ctx', 'head'), may hold values from -40 to 40
- log_decay: float32 [32, 16384], P('head', 'ctx'), may hold values from -2.5 to 0
- level_gate: float32 [32, 20, 16384], P('head', None, 'ctx'), may hold values from 0.2 to 2
- norm_gain: float32 [4096], P('head'), may hold values from 0.1 to 1.9
- attention_query: bfloat16 [16384, 4096], P('ctx', 'head'), may hold values from -170 to 170
- attention_key: bfloat16 [16384, 4096], P('ctx', 'head'), may hold values from -6.5 to 6.5
- attention_value: bfloat16 [16384, 4096], P('ctx', 'head'), may hold values from -6 to 6
Outputs:
- mixer_output: bfloat16 [16384, 4096], P('ctx', 'head')
- attention_output: bfloat16 [16384, 4096], P('ctx', 'head')
The draws below stay inside these ranges and needn't reach their ends.
All inputs are finite; a program needn't handle non-finite values.
Results may differ from the reference program's by a relative error of at most 0.0062.
Values may be sent and summed in bfloat16 or wider, within the bound.
A program may use at most 128 MiB of HBM per device.

```python
import math
import jax
import jax.numpy as jnp
from jax import lax

HEADS_PER_LAYER = 32
P_SIZE = 128
DS = 128
LEVELS = 20
WINDOW = 4
TOK_DEV = 512
SEQUENCE_TOKENS = 16384


def draw_state_gate(key, part):
    key = jax.random.fold_in(key, 11)
    noise_key, column_key = jax.random.split(key, 2)
    columns = jnp.arange(HEADS_PER_LAYER * P_SIZE, dtype=jnp.int32) // P_SIZE
    column_ramp = 3.0 ** (columns.astype(jnp.float32) / max(HEADS_PER_LAYER - 1, 1))
    spread = jnp.exp(jax.random.uniform(column_key, (HEADS_PER_LAYER * P_SIZE,), jnp.float32, 0.0, 1.2))
    values_drawn = jax.random.normal(noise_key, (SEQUENCE_TOKENS, HEADS_PER_LAYER * P_SIZE), jnp.float32) * (column_ramp * spread)[None, :]
    return jnp.clip(values_drawn, -40.0, 40.0).astype(jnp.bfloat16)


def draw_log_decay(key, part):
    key = jax.random.fold_in(key, 23)
    key_collection = jax.random.split(key, 7)
    fast_share = 0.5
    fast_heads = jax.random.uniform(key_collection[0], (HEADS_PER_LAYER,), jnp.float32) < fast_share
    fast_rate = jnp.exp(jax.random.uniform(key_collection[1], (HEADS_PER_LAYER,), jnp.float32, math.log(1.0 / 50.0), math.log(1.0 / 30.0)))
    slow_rate = 0.3 / SEQUENCE_TOKENS * jax.random.uniform(key_collection[2], (HEADS_PER_LAYER,), jnp.float32, 0.3, 1.0)
    baseline_decay_rate = jnp.where(fast_heads, fast_rate, slow_rate)
    token_multiplier = jnp.exp(jax.random.uniform(key_collection[3], (HEADS_PER_LAYER, SEQUENCE_TOKENS), jnp.float32, -0.7, 0.7))
    block_multiplier = jnp.exp(jax.random.uniform(key_collection[4], (HEADS_PER_LAYER, SEQUENCE_TOKENS // TOK_DEV), jnp.float32, -0.7, 0.7))
    block_multiplier = jnp.repeat(block_multiplier, TOK_DEV, axis=1)
    cluster_location = jax.random.randint(key_collection[5], (HEADS_PER_LAYER, 3), 0, SEQUENCE_TOKENS)
    cluster_depth = -jnp.log(1.0 - jax.random.uniform(key_collection[6], (HEADS_PER_LAYER, 3), jnp.float32, 0.2, 0.5))
    token_positions = jnp.arange(SEQUENCE_TOKENS, dtype=jnp.int32)
    token_clusters = jnp.sum(jnp.where(token_positions[None, None, :] == cluster_location[:, :, None], cluster_depth[:, :, None], 0.0), axis=1)
    return -(baseline_decay_rate[:, None] * token_multiplier * block_multiplier + token_clusters)


def attention_pair(key, boost):
    queries = jnp.clip(jax.random.normal(jax.random.fold_in(key, 101), (SEQUENCE_TOKENS, HEADS_PER_LAYER * P_SIZE), jnp.float32), -6.0, 6.0)
    keys_drawn = jnp.clip(jax.random.normal(jax.random.fold_in(key, 102), (SEQUENCE_TOKENS, HEADS_PER_LAYER * P_SIZE), jnp.float32), -6.0, 6.0)
    rows_index = jnp.arange(SEQUENCE_TOKENS, dtype=jnp.int32)
    picked = (rows_index % 97 == 50) & (rows_index >= 16) & (boost > 0.0)
    strength = jnp.where(rows_index // 97 % 3 == 0, 10.0, jnp.where(rows_index // 97 % 3 == 1, 18.0, 28.0))
    nudge = 2.0 / (strength * P_SIZE ** 0.5)
    twin_rows = jnp.roll(picked, -6)
    twin_nudge = jnp.roll(nudge, -6)
    keys_drawn = jnp.where(twin_rows[:, None], jnp.roll(keys_drawn, -3, axis=0) * (1.0 + twin_nudge[:, None]), keys_drawn)
    queries = jnp.where(picked[:, None], strength[:, None] * jnp.roll(keys_drawn, 3, axis=0), queries)
    return (queries, keys_drawn)


def draw_attention_query(key, part):
    boost = 0.0
    return attention_pair(key, boost)[0].astype(jnp.bfloat16)


def draw_attention_key(key, part):
    boost = 0.0
    return attention_pair(key, boost)[1].astype(jnp.bfloat16)


def level_of(stream_key, shape, pieces, low, largest):
    loudness, own = 1.0, jax.random.fold_in(stream_key, 6)
    for axis_at, blocks in pieces:
        heights = jnp.exp(jax.random.uniform(jax.random.fold_in(own, axis_at), (blocks,), jnp.float32, low / len(pieces), largest / len(pieces)))
        loudness = loudness * jnp.repeat(heights, shape[axis_at] // blocks).reshape([-1 if axis == axis_at else 1 for axis in range(len(shape))])
    return loudness


def scatter_about(stream_key, extent, deviation, most, cuts=(), kind=jnp.bfloat16):
    loudness = level_of(stream_key, extent, cuts, -0.22, 0.18) if cuts else 1.0
    array = jax.random.normal(stream_key, extent, jnp.float32) * deviation * loudness
    return jnp.minimum(jnp.maximum(array, -most), most).astype(kind)


def setup_inputs(seed: int = 0) -> dict:
    streams_of = jax.random.split(jax.random.key(seed), 11)
    return {
        "state_query": scatter_about(streams_of[0], (SEQUENCE_TOKENS, HEADS_PER_LAYER * DS), 1.0, 6.0, ((0, 32), (1, 8))),
        "state_key": scatter_about(streams_of[1], (SEQUENCE_TOKENS, HEADS_PER_LAYER * DS), DS ** -0.5, 0.5, ((0, 32), (1, 8))),
        "state_value": scatter_about(streams_of[2], (SEQUENCE_TOKENS, HEADS_PER_LAYER * P_SIZE), 1.0, 6.0, ((0, 32), (1, 8))),
        "state_gate": draw_state_gate(jax.random.fold_in(streams_of[10], 71), 0),
        "log_decay": draw_log_decay(jax.random.fold_in(streams_of[10], 71), 0),
        "level_gate": jnp.clip(jnp.exp(math.log(2.0) - 2.3025851 * jax.random.uniform(streams_of[5], (HEADS_PER_LAYER, LEVELS, SEQUENCE_TOKENS), jnp.float32) ** level_of(streams_of[5], (HEADS_PER_LAYER, LEVELS, SEQUENCE_TOKENS), ((0, 8), (2, 32)), -0.2, 0.2)), 0.2, 2.0),
        "norm_gain": jnp.clip(1.0 + 0.18 * jax.random.normal(streams_of[6], (HEADS_PER_LAYER * P_SIZE,), jnp.float32), 0.1, 1.9),
        "attention_query": draw_attention_query(jax.random.fold_in(streams_of[10], 71), 0),
        "attention_key": draw_attention_key(jax.random.fold_in(streams_of[10], 71), 0),
        "attention_value": scatter_about(streams_of[9], (SEQUENCE_TOKENS, HEADS_PER_LAYER * P_SIZE), 1.0, 6.0, ((0, 32), (1, 8))),
    }


highest = lax.Precision.HIGHEST

def bit_length(values):
    length_sum = jnp.zeros(values.shape, jnp.int32)
    for bit_index in range(LEVELS):
        length_sum = length_sum + (values >= 1 << bit_index).astype(jnp.int32)
    return length_sum

def rounded(values):
    return lax.optimization_barrier(values.astype(jnp.bfloat16)).astype(jnp.float32)

def reference(state_query, state_key, state_value, state_gate, log_decay, level_gate, norm_gain, attention_query, attention_key, attention_value):
    blocks = SEQUENCE_TOKENS // TOK_DEV
    shift_bits = TOK_DEV.bit_length() - 1
    block_levels = blocks.bit_length() - 1
    query_blocks = state_query.reshape(blocks, TOK_DEV, HEADS_PER_LAYER, DS)
    key_blocks = state_key.reshape(blocks, TOK_DEV, HEADS_PER_LAYER, DS)
    value_blocks = state_value.reshape(blocks, TOK_DEV, HEADS_PER_LAYER, P_SIZE)
    decay_blocks = log_decay.reshape(HEADS_PER_LAYER, blocks, TOK_DEV).transpose(1, 0, 2)
    gate_blocks = level_gate.reshape(HEADS_PER_LAYER, LEVELS, blocks, TOK_DEV).transpose(2, 0, 1, 3)
    token_positions = jnp.arange(TOK_DEV, dtype=jnp.int32)
    causal = token_positions[:, None] >= token_positions[None, :]
    pair_level = bit_length(jnp.bitwise_xor(token_positions[:, None], token_positions[None, :]))

    def inside_block(inputs):
        queries, keys_in, values_in, decays, gate_rows = inputs
        cum_decay = jnp.cumsum(decays, axis=1)
        scores = jnp.einsum('ihd,jhd->hij', queries.astype(jnp.float32), keys_in.astype(jnp.float32), precision=highest)
        decay_gap = jnp.where(causal[None], cum_decay[:, :, None] - cum_decay[:, None, :], -jnp.inf)
        level_scale = jnp.zeros(scores.shape, jnp.float32)
        for level_index in range(shift_bits + 1):
            level_scale = level_scale + jnp.where((pair_level == level_index)[None], gate_rows[:, level_index, :, None], 0.0)
        mixing = (scores * jnp.exp(decay_gap) * level_scale).astype(jnp.bfloat16)
        inside = jnp.einsum('hij,jhp->ihp', mixing.astype(jnp.float32), values_in.astype(jnp.float32), precision=highest)
        tail_decay = jnp.exp(cum_decay[:, -1:] - cum_decay)
        weighted_keys = rounded(keys_in.astype(jnp.float32) * tail_decay.T[:, :, None])
        block_state = jnp.einsum('jhd,jhp->hdp', weighted_keys, values_in.astype(jnp.float32), precision=highest)
        return (inside, block_state, cum_decay)
    inside_all, states, cum_blocks = lax.map(inside_block, (query_blocks, key_blocks, value_blocks, decay_blocks, gate_blocks))
    totals = cum_blocks[:, :, -1]
    block_ends = jnp.cumsum(totals, axis=0)
    starts = block_ends - totals
    block_ids = jnp.arange(blocks, dtype=jnp.int32)
    block_pair = bit_length(jnp.bitwise_xor(block_ids[:, None], block_ids[None, :]))

    def across_block(inputs):
        target, queries, cum_decay, gate_rows = inputs
        earlier = block_ids < target
        start_here = lax.dynamic_index_in_dim(starts, target, 0, keepdims=False)
        pair_here = lax.dynamic_index_in_dim(block_pair, target, 0, keepdims=False)
        decayed = jnp.exp(jnp.where(earlier[:, None], start_here[None, :] - block_ends, -jnp.inf))
        query_reach = rounded(queries.astype(jnp.float32) * jnp.exp(cum_decay).T[:, :, None])
        across = jnp.zeros((TOK_DEV, HEADS_PER_LAYER, P_SIZE), jnp.float32)
        for level_index in range(1, block_levels + 1):
            chosen = jnp.where((pair_here == level_index)[:, None], decayed, 0.0)
            level_state = rounded(jnp.einsum('sh,shdp->hdp', chosen, states, precision=highest))
            product = jnp.einsum('ihd,hdp->ihp', query_reach, level_state, precision=highest)
            across = across + product * gate_rows[:, shift_bits + level_index, :].T[:, :, None]
        return across
    across_all = lax.map(across_block, (block_ids, query_blocks, cum_blocks, gate_blocks))
    mixed_heads = (inside_all + across_all).reshape(SEQUENCE_TOKENS, HEADS_PER_LAYER * P_SIZE)
    gated_heads = mixed_heads * jax.nn.silu(state_gate.astype(jnp.float32))
    norm_scale = lax.rsqrt(lax.optimization_barrier(jnp.mean(gated_heads * gated_heads, axis=1, keepdims=True)) + 1e-05)
    mixer_output = (gated_heads * norm_scale * norm_gain[None, :]).astype(jnp.bfloat16)
    pad_rows = (WINDOW - 1) * TOK_DEV
    padded_keys = jnp.concatenate([jnp.zeros((pad_rows, HEADS_PER_LAYER * P_SIZE), jnp.bfloat16), attention_key], axis=0)
    padded_values = jnp.concatenate([jnp.zeros((pad_rows, HEADS_PER_LAYER * P_SIZE), jnp.bfloat16), attention_value], axis=0)

    def attend(block_index):
        first_row = block_index * TOK_DEV
        query_block = lax.dynamic_slice_in_dim(attention_query, first_row, TOK_DEV, 0).reshape(TOK_DEV, HEADS_PER_LAYER, P_SIZE)
        key_window = lax.dynamic_slice_in_dim(padded_keys, first_row, WINDOW * TOK_DEV, 0).reshape(WINDOW * TOK_DEV, HEADS_PER_LAYER, P_SIZE)
        value_window = lax.dynamic_slice_in_dim(padded_values, first_row, WINDOW * TOK_DEV, 0).reshape(WINDOW * TOK_DEV, HEADS_PER_LAYER, P_SIZE)
        key_positions = first_row - pad_rows + jnp.arange(WINDOW * TOK_DEV, dtype=jnp.int32)
        query_positions = first_row + token_positions
        allowed = (key_positions[None, :] >= 0) & (key_positions[None, :] <= query_positions[:, None])
        logits = jnp.einsum('ihd,jhd->hij', query_block.astype(jnp.float32), key_window.astype(jnp.float32), precision=highest) * (1.0 / math.sqrt(P_SIZE))
        logits = jnp.where(allowed[None], logits, -jnp.inf)
        row_max = lax.optimization_barrier(jnp.max(logits, axis=2, keepdims=True))
        exponent = jnp.exp(logits - row_max)
        weights_low = (exponent / lax.optimization_barrier(jnp.sum(exponent, axis=2, keepdims=True))).astype(jnp.bfloat16)
        attended = jnp.einsum('hij,jhd->ihd', weights_low.astype(jnp.float32), value_window.astype(jnp.float32), precision=highest)
        return attended.reshape(TOK_DEV, HEADS_PER_LAYER * P_SIZE).astype(jnp.bfloat16)
    attention_output = lax.map(attend, jnp.arange(blocks, dtype=jnp.int32)).reshape(SEQUENCE_TOKENS, HEADS_PER_LAYER * P_SIZE)
    return (mixer_output, attention_output)
```

```python
import functools
import math

import jax
import jax.numpy as jnp
from jax import lax
from jax.experimental import pallas as pl
from jax.experimental.pallas import tpu as pltpu
from jax.sharding import PartitionSpec as P

MESH = pl.DeviceIdType.MESH
ROW = 4
F32 = jnp.float32
BF16 = jnp.bfloat16
NEG = -1e30


def nt_dot(a, b):
    return lax.dot_general(a, b, (((1,), (1,)), ((), ())), preferred_element_type=F32)


def tn_dot(a, b):
    return lax.dot_general(a, b, (((0,), (0,)), ((), ())), preferred_element_type=F32)


def kernel(
    zn,
    hn,
    sq_hbm,
    sk_hbm,
    sv_hbm,
    sg_hbm,
    ld_ref,
    lg_ref,
    gain_ref,
    aq_hbm,
    ak_hbm,
    av_hbm,
    mo_hbm,
    ao_hbm,
    sq,
    sk,
    sv,
    sg,
    qbuf,
    kbuf,
    vbuf,
    obuf,
    grow,
    gcol,
    mixed,
    gated,
    mout,
    ssend,
    srecv,
    tsend,
    trecv,
    rsend,
    rrecv,
    trsend,
    trrecv,
    lsend,
    lrecv,
    nsend,
    nrecv,
    loc_sem,
    x_send,
    x_recv,
    h_send,
    h_recv,
    s_send,
    s_recv,
    r_send,
    r_recv,
    l_send,
    l_recv,
    n_send,
    n_recv,
    o_send,
    o_recv,
    out_sem,
):
    me = lax.axis_index("ctx")
    mh = lax.axis_index("head")
    z = me // ROW
    x = me % ROW
    tok = qbuf.shape[1]
    hd = qbuf.shape[2]
    chunk = 128
    chunks = tok // chunk

    def rowdev(d):
        return z * ROW + (x + d) % ROW

    def cols(h):
        return pl.ds(pl.multiple_of(h * hd, hd), hd)

    state_in = [
        pltpu.make_async_copy(src, dst, loc_sem.at[i])
        for i, (src, dst) in enumerate(((sk_hbm, sk), (sv_hbm, sv), (sq_hbm, sq), (sg_hbm, sg)))
    ]
    for c in state_in:
        c.start()
    att = ((ak_hbm, kbuf, 3), (av_hbm, vbuf, 3), (aq_hbm, qbuf, 0))
    own_in = [
        pltpu.make_async_copy(src.at[:, cols(x)], dst.at[base + x], loc_sem.at[4 + i])
        for i, (src, dst, base) in enumerate(att)
    ]
    for c in own_in:
        c.start()

    rrecv[...] = jnp.zeros_like(rrecv)
    trrecv[...] = jnp.zeros_like(trrecv)

    @pl.when(x != 3)
    def _():
        lrecv[:, 4] = jnp.zeros_like(lrecv[:, 4])

    @pl.when(z == 0)
    def _():
        kbuf[0:3] = jnp.zeros((3, tok, hd), BF16)
        vbuf[0:3] = jnp.zeros((3, tok, hd), BF16)

    barrier = pltpu.get_barrier_semaphore()
    for d in range(1, ROW):
        pl.semaphore_signal(barrier, inc=1, device_id={"ctx": rowdev(d)}, device_id_type=MESH)
    for d in range(1, zn):
        pl.semaphore_signal(
            barrier, inc=1, device_id={"ctx": ((z + d) % zn) * ROW + x}, device_id_type=MESH
        )
    for d in range(1, hn):
        pl.semaphore_signal(barrier, inc=1, device_id={"head": (mh + d) % hn}, device_id_type=MESH)
    pl.semaphore_wait(barrier, ROW - 1 + zn - 1 + hn - 1)

    def x_copy(t, d):
        src, dst, base = att[t]
        return pltpu.make_async_remote_copy(
            src_ref=src.at[:, cols((x + d) % ROW)],
            dst_ref=dst.at[base + x],
            send_sem=x_send.at[t, d - 1],
            recv_sem=x_recv.at[t, d - 1],
            device_id={"ctx": rowdev(d)},
            device_id_type=MESH,
        )

    def x_wait(t, d):
        src, dst, base = att[t]
        pltpu.make_async_remote_copy(
            src_ref=src.at[:, cols((x + d) % ROW)],
            dst_ref=dst.at[base + (x + ROW - d) % ROW],
            send_sem=x_send.at[t, d - 1],
            recv_sem=x_recv.at[t, d - 1],
            device_id={"ctx": rowdev(d)},
            device_id_type=MESH,
        ).wait_recv()

    def halo_own(t):
        src, dst, _ = att[t]
        return pltpu.make_async_remote_copy(
            src_ref=src.at[:, cols(x)],
            dst_ref=dst.at[(x + ROW - 1) % ROW],
            send_sem=h_send.at[t, 0],
            recv_sem=h_recv.at[t, (x + ROW - 1) % ROW],
            device_id={"ctx": me + ROW},
            device_id_type=MESH,
        )

    def halo_relay(t, d):
        dst = att[t][1]
        block = (x + ROW - d) % ROW
        return pltpu.make_async_remote_copy(
            src_ref=dst.at[3 + block],
            dst_ref=dst.at[(block + ROW - 1) % ROW],
            send_sem=h_send.at[t, d],
            recv_sem=h_recv.at[t, (block + ROW - 1) % ROW],
            device_id={"ctx": me + ROW},
            device_id_type=MESH,
        )

    def relay_if(d):
        return ((x + ROW - d) % ROW >= 1) & (z < zn - 1)

    def halo_wait(t, slot):
        dst = att[t][1]
        pltpu.make_async_remote_copy(
            src_ref=dst.at[slot],
            dst_ref=dst.at[slot],
            send_sem=h_send.at[t, 0],
            recv_sem=h_recv.at[t, slot],
            device_id={"ctx": (me + ROW) % (zn * ROW)},
            device_id_type=MESH,
        ).wait_recv()

    def s_copies(d):
        p = (x + d) % ROW
        return [
            pltpu.make_async_remote_copy(
                src_ref=src.at[p],
                dst_ref=dst.at[x],
                send_sem=s_send.at[i, d - 1],
                recv_sem=s_recv.at[i, d - 1],
                device_id={"ctx": rowdev(d)},
                device_id_type=MESH,
            )
            for i, (src, dst) in enumerate(((ssend, srecv), (tsend, trecv)))
        ]

    def r_copies(d):
        return [
            pltpu.make_async_remote_copy(
                src_ref=src,
                dst_ref=dst.at[d - 1],
                send_sem=r_send.at[i, d - 1],
                recv_sem=r_recv.at[i, d - 1],
                device_id={"ctx": ((z + d) % zn) * ROW + x},
                device_id_type=MESH,
            )
            for i, (src, dst) in enumerate(((rsend, rrecv), (trsend, trrecv)))
        ]

    def l_copy(i, d):
        part = pl.ds(0, 4) if i == 0 else pl.ds(4, 1)
        return pltpu.make_async_remote_copy(
            src_ref=lsend.at[d, part],
            dst_ref=lrecv.at[x, part],
            send_sem=l_send.at[i, d - 1],
            recv_sem=l_recv.at[i, d - 1],
            device_id={"ctx": rowdev(d)},
            device_id_type=MESH,
        )

    def n_copy(d):
        return pltpu.make_async_remote_copy(
            src_ref=nsend,
            dst_ref=nrecv.at[d - 1],
            send_sem=n_send.at[d - 1],
            recv_sem=n_recv.at[d - 1],
            device_id={"head": (mh + d) % hn},
            device_id_type=MESH,
        )

    def o_copy(j):
        return pltpu.make_async_remote_copy(
            src_ref=obuf.at[j],
            dst_ref=ao_hbm.at[:, cols(x)],
            send_sem=o_send.at[j],
            recv_sem=o_recv.at[x],
            device_id={"ctx": z * ROW + j},
            device_id_type=MESH,
        )

    def o_local(j):
        return pltpu.make_async_copy(obuf.at[j], ao_hbm.at[:, cols(x)], out_sem.at[1])

    for d in (1, 3, 2):
        x_copy(0, d).start()
    own_halo = (x >= 1) & (z < zn - 1)

    @pl.when(own_halo)
    def _():
        halo_own(0).start()
        halo_own(1).start()

    lane = lax.broadcasted_iota(jnp.int32, (8, tok), 1)
    cum = jnp.concatenate([ld_ref[...], jnp.zeros((8 - ROW, tok), F32)], axis=0)
    shift = 1
    while shift < tok:
        cum = cum + jnp.where(lane >= shift, pltpu.roll(cum, shift, axis=1), 0.0)
        shift *= 2
    last = cum[:, tok - 1 : tok]
    tail = jnp.exp(last - cum)
    reach = jnp.exp(cum)
    for h in range(ROW):
        grow[h, 0:20, :] = lg_ref[h]
        grow[h, 20:21, :] = cum[h : h + 1]
        grow[h, 21:22, :] = tail[h : h + 1]
        grow[h, 22:23, :] = reach[h : h + 1]
        grow[h, 23:24, :] = cum[h : h + 1]
        grow[h, 24:32, :] = cum
        tsend[h] = jnp.broadcast_to(last[h : h + 1], (8, 128))
        gcol[h] = grow[h].T

    state_in[0].wait()
    state_in[1].wait()

    def summary(h, _):
        kf = sk[:, cols(h)].astype(F32)
        low = (kf * gcol[h, :, 21:22]).astype(BF16)
        ssend[h] = tn_dot(low, sv[:, cols(h)]).astype(BF16)
        return 0

    lax.fori_loop(0, ROW, summary, 0)
    for d in (1, 3, 2):
        for c in s_copies(d):
            c.start()
    for t in (1, 2):
        for d in (1, 3, 2):
            x_copy(t, d).start()
    srecv[x] = ssend[x]
    trecv[x] = tsend[x]

    state_in[2].wait()
    state_in[3].wait()
    row_i = lax.broadcasted_iota(jnp.int32, (chunk, chunk), 0)
    col_i = lax.broadcasted_iota(jnp.int32, (chunk, chunk), 1)

    apart = row_i ^ col_i

    def inside(h, _):
        hc = cols(h)
        crow = grow[h, 20:21, :]
        for i in range(chunks):
            rows = pl.ds(i * chunk, chunk)
            g = gcol[h, rows, :]
            ccol = g[:, 20:21]
            scores = nt_dot(sq[rows, hc], sk[0 : (i + 1) * chunk, hc])
            parts = []
            for j in range(i + 1):
                s = scores[:, j * chunk : (j + 1) * chunk]
                gap = ccol - crow[:, j * chunk : (j + 1) * chunk]
                if j < i:
                    level = (i ^ j).bit_length() + 7
                    m = s * jnp.exp(gap) * g[:, level : level + 1]
                else:
                    gate = jnp.broadcast_to(g[:, 0:1], (chunk, chunk))
                    for level in range(1, 8):
                        gate = jnp.where(apart >= 1 << (level - 1), g[:, level : level + 1], gate)
                    seen = row_i >= col_i
                    m = jnp.where(seen, s * jnp.exp(jnp.where(seen, gap, 0.0)) * gate, 0.0)
                parts.append(m.astype(BF16))
            low = parts[0] if i == 0 else jnp.concatenate(parts, axis=1)
            mixed[h, rows, :] = jnp.dot(
                low, sv[0 : (i + 1) * chunk, hc], preferred_element_type=F32
            )
        return 0

    lax.fori_loop(0, ROW, inside, 0)

    for d in range(1, ROW):
        p = (x + ROW - d) % ROW
        for i, (src, dst) in enumerate(((ssend, srecv), (tsend, trecv))):
            pltpu.make_async_remote_copy(
                src_ref=src.at[p],
                dst_ref=dst.at[p],
                send_sem=s_send.at[i, d - 1],
                recv_sem=s_recv.at[i, d - 1],
                device_id={"ctx": rowdev(d)},
                device_id_type=MESH,
            ).wait_recv()
    tot = [trecv[i] for i in range(ROW)]
    st = [srecv[i].astype(F32) for i in range(ROW)]
    pair = st[0] * jnp.exp(tot[1][0:1]) + st[1]
    row_state = (
        pair * jnp.exp((tot[2] + tot[3])[0:1]) + st[2] * jnp.exp(tot[3][0:1]) + st[3]
    )
    rsend[...] = row_state.astype(BF16)
    trsend[...] = tot[0] + tot[1] + tot[2] + tot[3]
    for d in range(1, zn):

        @pl.when(z + d < zn)
        def _():
            for c in r_copies(d):
                c.start()

    for c in own_in:
        c.wait()
    for d in (1, 3, 2):
        for t in (0, 1):
            x_wait(t, d)

            @pl.when(relay_if(d))
            def _():
                halo_relay(t, d).start()

    for d in (1, 3, 2):
        x_wait(2, d)

    kappa = math.log2(math.e) / math.sqrt(hd)
    qrows = 256
    absent = jnp.where(z == 0, NEG, 0.0).astype(F32)

    def attend(j):
        def body(i, _):
            first = pl.multiple_of(i * qrows, qrows)
            q = qbuf[j, pl.ds(first, qrows), :]
            logits = []
            for s in range(ROW):
                part = nt_dot(q, kbuf[j + s])
                if j + s < 3:
                    part = part + absent
                if s == ROW - 1:
                    r = lax.broadcasted_iota(jnp.int32, (qrows, tok), 0) + first
                    c = lax.broadcasted_iota(jnp.int32, (qrows, tok), 1)
                    part = jnp.where(r >= c, part, NEG)
                logits.append(part)
            top = jnp.maximum(
                jnp.maximum(logits[0], logits[1]), jnp.maximum(logits[2], logits[3])
            )
            top = jnp.max(top, axis=1, keepdims=True)
            weights = [jnp.exp2((part - top) * kappa) for part in logits]
            total = jnp.sum(
                (weights[0] + weights[1]) + (weights[2] + weights[3]), axis=1, keepdims=True
            )
            out = None
            for s in range(ROW):
                term = jnp.dot(
                    weights[s].astype(BF16), vbuf[j + s], preferred_element_type=F32
                )
                out = term if out is None else out + term
            obuf[j, pl.ds(first, qrows), :] = (out / total).astype(BF16)
            return 0

        lax.fori_loop(0, tok // qrows, body, 0)

        @pl.when(x != j)
        def _():
            o_copy(j).start()

        @pl.when(x == j)
        def _():
            o_local(j).start()

    attend(3)

    for d in range(1, zn):

        @pl.when(z - d >= 0)
        def _():
            for c in r_copies(d):
                c.wait_recv()

    levels = [jnp.zeros((hd, hd), F32) for _ in range(3)]
    decay = jnp.zeros((8, 128), F32)
    for d in range(1, zn):
        other = z + zn - d
        near2 = (z + zn) // 2 == other // 2
        near4 = (z + zn) // 4 == other // 4
        w = jnp.exp(decay)[0:1]
        held = rrecv[d - 1].astype(F32)
        levels[0] = levels[0] + jnp.where(near2, w, 0.0) * held
        levels[1] = levels[1] + jnp.where(near4 & ~near2, w, 0.0) * held
        levels[2] = levels[2] + jnp.where(near4, 0.0, w) * held
        decay = decay + trrecv[d - 1]
    for d in (0, 1, 3, 2):
        xp = (x + d) % ROW
        before = (
            jnp.where(xp >= 1, tot[0], 0.0)
            + jnp.where(xp >= 2, tot[1], 0.0)
            + jnp.where(xp >= 3, tot[2], 0.0)
        )
        w = jnp.exp(before)[0:1]
        for m in range(3):
            lsend[d, m] = (levels[m] * w).astype(BF16)
        near = jnp.where(xp == 1, st[0], jnp.where(xp == 2, pair, jnp.where(xp == 3, st[2], 0.0)))
        lsend[d, 3] = near.astype(BF16)
        lsend[d, 4] = (pair * jnp.exp(tot[2][0:1])).astype(BF16)
        if d > 0:
            l_copy(0, d).start()

            @pl.when(xp == 3)
            def _():
                l_copy(1, d).start()

    lrecv[x, 0:4] = lsend[0, 0:4]

    @pl.when(x == 3)
    def _():
        lrecv[x, 4] = lsend[0, 4]

    def halos(slot):
        @pl.when(z > 0)
        def _():
            for t in (0, 1):
                halo_wait(t, slot)

    halos(2)
    attend(2)

    for d in range(1, ROW):
        p = (x + ROW - d) % ROW
        pltpu.make_async_remote_copy(
            src_ref=lsend.at[d, pl.ds(0, 4)],
            dst_ref=lrecv.at[p, pl.ds(0, 4)],
            send_sem=l_send.at[0, d - 1],
            recv_sem=l_recv.at[0, d - 1],
            device_id={"ctx": rowdev(d)},
            device_id_type=MESH,
        ).wait_recv()

        @pl.when(x == 3)
        def _():
            pltpu.make_async_remote_copy(
                src_ref=lsend.at[d, pl.ds(4, 1)],
                dst_ref=lrecv.at[p, pl.ds(4, 1)],
                send_sem=l_send.at[1, d - 1],
                recv_sem=l_recv.at[1, d - 1],
                device_id={"ctx": rowdev(d)},
                device_id_type=MESH,
            ).wait_recv()

    def across(h, acc):
        hc = cols(h)
        squares = []
        for i in range(chunks):
            rows = pl.ds(i * chunk, chunk)
            g = gcol[h, rows, :]
            qf = sq[rows, hc].astype(F32) * g[:, 22:23]
            near = jnp.where(x == 2, g[:, 11:12], g[:, 10:11])
            low = jnp.concatenate(
                [
                    (qf * gate).astype(BF16)
                    for gate in (g[:, 12:13], g[:, 13:14], g[:, 14:15], near, g[:, 11:12])
                ],
                axis=1,
            )
            far = jnp.dot(low, lrecv[h].reshape(5 * hd, hd), preferred_element_type=F32)
            v = sg[rows, hc].astype(F32)
            out = (mixed[h, rows, :] + far) * (v / (1.0 + jnp.exp(-v)))
            gated[rows, hc] = out
            squares.append(out * out)
        return tuple(a + s for a, s in zip(acc, squares))

    acc = lax.fori_loop(
        0, ROW, across, tuple(jnp.zeros((chunk, hd), F32) for _ in range(chunks))
    )
    nsend[...] = jnp.zeros_like(nsend)
    for i in range(chunks):
        nsend[i : i + 1, :] = jnp.sum(acc[i].T, axis=0, keepdims=True)
    for d in range(1, hn):
        n_copy(d).start()

    halos(1)
    attend(1)
    halos(0)
    attend(0)

    total = nsend[...]
    for d in range(1, hn):
        n_copy(d).wait_recv()
        total = total + nrecv[d - 1]
    scale = lax.rsqrt(total / (hn * ROW * hd) + 1e-05)
    for i in range(chunks):
        rows = pl.ds(i * chunk, chunk)
        scale_col = jnp.broadcast_to(scale[i : i + 1], (chunk, chunk)).T
        for h in range(ROW):
            hs = slice(h * hd, (h + 1) * hd)
            mout[rows, hs] = (gated[rows, hs] * scale_col * gain_ref[:, hs]).astype(BF16)
    mix_out = pltpu.make_async_copy(mout, mo_hbm, out_sem.at[0])
    mix_out.start()

    for d in range(1, ROW):
        for t in range(3):
            x_copy(t, d).wait_send()
        for c in s_copies(d):
            c.wait_send()
        l_copy(0, d).wait_send()

        @pl.when((x + d) % ROW == 3)
        def _():
            l_copy(1, d).wait_send()

        @pl.when(relay_if(d))
        def _():
            for t in (0, 1):
                halo_relay(t, d).wait_send()

    @pl.when(own_halo)
    def _():
        for t in (0, 1):
            halo_own(t).wait_send()

    for d in range(1, zn):

        @pl.when(z + d < zn)
        def _():
            for c in r_copies(d):
                c.wait_send()

    for d in range(1, hn):
        n_copy(d).wait_send()
    for j in range(ROW):

        @pl.when(x != j)
        def _():
            o_copy(j).wait_send()
            pltpu.make_async_remote_copy(
                src_ref=obuf.at[j],
                dst_ref=ao_hbm.at[:, cols(j)],
                send_sem=o_send.at[j],
                recv_sem=o_recv.at[j],
                device_id={"ctx": z * ROW + j},
                device_id_type=MESH,
            ).wait_recv()

        @pl.when(x == j)
        def _():
            o_local(j).wait()

    mix_out.wait()


def shards(zn, hn, sq, sk, sv, sg, ld, lg, gain, aq, ak, av):
    tok = sq.shape[0]
    heads = ld.shape[0]
    hd = sq.shape[1] // heads
    wide = heads * hd
    dma = pltpu.SemaphoreType.DMA
    vm = pltpu.VMEM
    anywhere = pl.BlockSpec(memory_space=pl.ANY)
    here = pl.BlockSpec(memory_space=pltpu.VMEM)
    out = jax.ShapeDtypeStruct((tok, wide), BF16)
    return pl.pallas_call(
        functools.partial(kernel, zn, hn),
        out_shape=(out, out),
        in_specs=[anywhere] * 4 + [here] * 3 + [anywhere] * 3,
        out_specs=(anywhere, anywhere),
        scratch_shapes=[
            vm((tok, wide), BF16),
            vm((tok, wide), BF16),
            vm((tok, wide), BF16),
            vm((tok, wide), BF16),
            vm((4, tok, hd), BF16),
            vm((7, tok, hd), BF16),
            vm((7, tok, hd), BF16),
            vm((4, tok, hd), BF16),
            vm((heads, 32, tok), F32),
            vm((heads, tok, 32), F32),
            vm((heads, tok, hd), F32),
            vm((tok, wide), F32),
            vm((tok, wide), BF16),
            vm((4, hd, hd), BF16),
            vm((4, hd, hd), BF16),
            vm((4, 8, 128), F32),
            vm((4, 8, 128), F32),
            vm((hd, hd), BF16),
            vm((max(zn - 1, 1), hd, hd), BF16),
            vm((8, 128), F32),
            vm((max(zn - 1, 1), 8, 128), F32),
            vm((4, 5, hd, hd), BF16),
            vm((4, 5, hd, hd), BF16),
            vm((8, 128), F32),
            vm((max(hn - 1, 1), 8, 128), F32),
            dma((7,)),
            dma((3, 3)),
            dma((3, 3)),
            dma((2, 4)),
            dma((2, 4)),
            dma((2, 3)),
            dma((2, 3)),
            dma((2, max(zn - 1, 1))),
            dma((2, max(zn - 1, 1))),
            dma((2, 3)),
            dma((2, 3)),
            dma((max(hn - 1, 1),)),
            dma((max(hn - 1, 1),)),
            dma((4,)),
            dma((4,)),
            dma((2,)),
        ],
        compiler_params=pltpu.CompilerParams(
            collective_id=0, has_side_effects=True, vmem_limit_bytes=48 * 1024 * 1024
        ),
        cost_estimate=pl.CostEstimate(
            flops=3_000_000_000, bytes_accessed=5_000_000, transcendentals=5_000_000
        ),
    )(sq, sk, sv, sg, ld, lg, gain.reshape(1, wide), aq, ak, av)


def solution(mesh):
    zn = mesh.shape["ctx"] // ROW
    hn = mesh.shape["head"]
    return jax.shard_map(
        functools.partial(shards, zn, hn),
        mesh=mesh,
        in_specs=(
            P("ctx", "head"),
            P("ctx", "head"),
            P("ctx", "head"),
            P("ctx", "head"),
            P("head", "ctx"),
            P("head", None, "ctx"),
            P("head"),
            P("ctx", "head"),
            P("ctx", "head"),
            P("ctx", "head"),
        ),
        out_specs=(P("ctx", "head"), P("ctx", "head")),
        check_vma=False,
    )
```

```python
import functools
import math

import jax
import jax.numpy as jnp
from jax import lax
from jax.experimental import pallas as pl
from jax.experimental.pallas import tpu as pltpu
from jax.sharding import PartitionSpec as P

MESH = pl.DeviceIdType.MESH
ROW = 4
F32 = jnp.float32
BF16 = jnp.bfloat16
NEG = -1e30


def nt_dot(a, b):
    return lax.dot_general(a, b, (((1,), (1,)), ((), ())), preferred_element_type=F32)


def tn_dot(a, b):
    return lax.dot_general(a, b, (((0,), (0,)), ((), ())), preferred_element_type=F32)


def kernel(
    zn,
    hn,
    sq_hbm,
    sk_hbm,
    sv_hbm,
    sg_hbm,
    ld_ref,
    lg_hbm,
    gain_ref,
    aq_hbm,
    ak_hbm,
    av_hbm,
    mo_hbm,
    ao_hbm,
    sq,
    sk,
    sv,
    sg,
    qbuf,
    kbuf,
    vbuf,
    obuf,
    lgbuf,
    grow,
    gcol,
    mixed,
    gated,
    reached,
    mout,
    ssend,
    srecv,
    tsend,
    trecv,
    rsend,
    rrecv,
    trsend,
    trrecv,
    lsend,
    lrecv,
    nsend,
    nrecv,
    loc_sem,
    x_send,
    x_recv,
    h_send,
    h_recv,
    s_send,
    s_recv,
    r_send,
    r_recv,
    l_send,
    l_recv,
    n_send,
    n_recv,
    o_send,
    o_recv,
    out_sem,
):
    me = lax.axis_index("ctx")
    mh = lax.axis_index("head")
    z = me // ROW
    x = me % ROW
    tok = qbuf.shape[1]
    hd = qbuf.shape[2]
    chunk = 128
    chunks = tok // chunk

    def rowdev(d):
        return z * ROW + (x + d) % ROW

    def cols(h):
        return pl.ds(pl.multiple_of(h * hd, hd), hd)

    state_in = [
        pltpu.make_async_copy(src, dst, loc_sem.at[i])
        for i, (src, dst) in enumerate(((sk_hbm, sk), (sv_hbm, sv), (sq_hbm, sq), (sg_hbm, sg)))
    ]
    gates_in = pltpu.make_async_copy(lg_hbm, lgbuf, loc_sem.at[7])
    gates_in.start()
    for c in state_in:
        c.start()
    att = ((ak_hbm, kbuf, 3), (av_hbm, vbuf, 3), (aq_hbm, qbuf, 0))
    own_in = [
        pltpu.make_async_copy(src.at[:, cols(x)], dst.at[base + x], loc_sem.at[4 + i])
        for i, (src, dst, base) in enumerate(att)
    ]
    for c in own_in:
        c.start()

    rrecv[...] = jnp.zeros_like(rrecv)
    trrecv[...] = jnp.zeros_like(trrecv)

    @pl.when(x != 3)
    def _():
        lrecv[:, 4] = jnp.zeros_like(lrecv[:, 4])

    @pl.when(z == 0)
    def _():
        kbuf[0:3] = jnp.zeros((3, tok, hd), BF16)
        vbuf[0:3] = jnp.zeros((3, tok, hd), BF16)

    barrier = pltpu.get_barrier_semaphore()
    for d in range(1, ROW):
        pl.semaphore_signal(barrier, inc=1, device_id={"ctx": rowdev(d)}, device_id_type=MESH)
    for d in range(1, zn):
        pl.semaphore_signal(
            barrier, inc=1, device_id={"ctx": ((z + d) % zn) * ROW + x}, device_id_type=MESH
        )
    for d in range(1, hn):
        pl.semaphore_signal(barrier, inc=1, device_id={"head": (mh + d) % hn}, device_id_type=MESH)

    def x_copy(t, d):
        src, dst, base = att[t]
        return pltpu.make_async_remote_copy(
            src_ref=src.at[:, cols((x + d) % ROW)],
            dst_ref=dst.at[base + x],
            send_sem=x_send.at[t, d - 1],
            recv_sem=x_recv.at[t, d - 1],
            device_id={"ctx": rowdev(d)},
            device_id_type=MESH,
        )

    def x_wait(t, d):
        src, dst, base = att[t]
        pltpu.make_async_remote_copy(
            src_ref=src.at[:, cols((x + d) % ROW)],
            dst_ref=dst.at[base + (x + ROW - d) % ROW],
            send_sem=x_send.at[t, d - 1],
            recv_sem=x_recv.at[t, d - 1],
            device_id={"ctx": rowdev(d)},
            device_id_type=MESH,
        ).wait_recv()

    def halo_own(t):
        src, dst, _ = att[t]
        return pltpu.make_async_remote_copy(
            src_ref=src.at[:, cols(x)],
            dst_ref=dst.at[(x + ROW - 1) % ROW],
            send_sem=h_send.at[t, 0],
            recv_sem=h_recv.at[t, (x + ROW - 1) % ROW],
            device_id={"ctx": me + ROW},
            device_id_type=MESH,
        )

    def halo_relay(t, d):
        dst = att[t][1]
        block = (x + ROW - d) % ROW
        return pltpu.make_async_remote_copy(
            src_ref=dst.at[3 + block],
            dst_ref=dst.at[(block + ROW - 1) % ROW],
            send_sem=h_send.at[t, d],
            recv_sem=h_recv.at[t, (block + ROW - 1) % ROW],
            device_id={"ctx": me + ROW},
            device_id_type=MESH,
        )

    def relay_if(d):
        return ((x + ROW - d) % ROW >= 1) & (z < zn - 1)

    def halo_wait(t, slot):
        dst = att[t][1]
        pltpu.make_async_remote_copy(
            src_ref=dst.at[slot],
            dst_ref=dst.at[slot],
            send_sem=h_send.at[t, 0],
            recv_sem=h_recv.at[t, slot],
            device_id={"ctx": (me + ROW) % (zn * ROW)},
            device_id_type=MESH,
        ).wait_recv()

    def s_copies(d):
        p = (x + d) % ROW
        return [
            pltpu.make_async_remote_copy(
                src_ref=src.at[p],
                dst_ref=dst.at[x],
                send_sem=s_send.at[i, d - 1],
                recv_sem=s_recv.at[i, d - 1],
                device_id={"ctx": rowdev(d)},
                device_id_type=MESH,
            )
            for i, (src, dst) in enumerate(((ssend, srecv), (tsend, trecv)))
        ]

    def r_copies(d):
        return [
            pltpu.make_async_remote_copy(
                src_ref=src,
                dst_ref=dst.at[d - 1],
                send_sem=r_send.at[i, d - 1],
                recv_sem=r_recv.at[i, d - 1],
                device_id={"ctx": ((z + d) % zn) * ROW + x},
                device_id_type=MESH,
            )
            for i, (src, dst) in enumerate(((rsend, rrecv), (trsend, trrecv)))
        ]

    def l_copy(i, d):
        part = pl.ds(0, 4) if i == 0 else pl.ds(4, 1)
        return pltpu.make_async_remote_copy(
            src_ref=lsend.at[d, part],
            dst_ref=lrecv.at[x, part],
            send_sem=l_send.at[i, d - 1],
            recv_sem=l_recv.at[i, d - 1],
            device_id={"ctx": rowdev(d)},
            device_id_type=MESH,
        )

    def n_copy(d):
        return pltpu.make_async_remote_copy(
            src_ref=nsend,
            dst_ref=nrecv.at[d - 1],
            send_sem=n_send.at[d - 1],
            recv_sem=n_recv.at[d - 1],
            device_id={"head": (mh + d) % hn},
            device_id_type=MESH,
        )

    def o_copy(j):
        return pltpu.make_async_remote_copy(
            src_ref=obuf.at[j],
            dst_ref=ao_hbm.at[:, cols(x)],
            send_sem=o_send.at[j],
            recv_sem=o_recv.at[x],
            device_id={"ctx": z * ROW + j},
            device_id_type=MESH,
        )

    def o_local(j):
        return pltpu.make_async_copy(obuf.at[j], ao_hbm.at[:, cols(x)], out_sem.at[1])

    lane = lax.broadcasted_iota(jnp.int32, (8, tok), 1)
    cum = jnp.concatenate([ld_ref[...], jnp.zeros((8 - ROW, tok), F32)], axis=0)
    shift = 1
    while shift < tok:
        cum = cum + jnp.where(lane >= shift, pltpu.roll(cum, shift, axis=1), 0.0)
        shift *= 2
    last = cum[:, tok - 1 : tok]
    tail = jnp.exp(last - cum)
    reach = jnp.exp(cum)
    gates_in.wait()
    for h in range(ROW):
        grow[h, 0:20, :] = lgbuf[:, h, :]
        grow[h, 20:21, :] = cum[h : h + 1]
        grow[h, 21:22, :] = tail[h : h + 1]
        grow[h, 22:23, :] = reach[h : h + 1]
        grow[h, 23:24, :] = cum[h : h + 1]
        grow[h, 24:32, :] = cum
        tsend[h] = jnp.broadcast_to(last[h : h + 1], (8, 128))
        gcol[h] = grow[h].T

    pl.semaphore_wait(barrier, ROW - 1 + zn - 1 + hn - 1)

    for d in (1, 3):
        x_copy(0, d).start()
    own_halo = (x >= 1) & (z < zn - 1)

    @pl.when(own_halo)
    def _():
        halo_own(0).start()
        halo_own(1).start()

    state_in[0].wait()
    state_in[1].wait()

    def summary(h, _):
        kf = sk[:, cols(h)].astype(F32)
        low = (kf * gcol[h, :, 21:22]).astype(BF16)
        ssend[h] = tn_dot(low, sv[:, cols(h)]).astype(BF16)
        return 0

    lax.fori_loop(0, ROW, summary, 0)
    for d in (1, 3, 2):
        for c in s_copies(d):
            c.start()
    for t, d in ((1, 1), (1, 3), (0, 2), (1, 2), (2, 1), (2, 3), (2, 2)):
        x_copy(t, d).start()
    srecv[x] = ssend[x]
    trecv[x] = tsend[x]

    state_in[2].wait()
    state_in[3].wait()
    row_i = lax.broadcasted_iota(jnp.int32, (chunk, chunk), 0)
    col_i = lax.broadcasted_iota(jnp.int32, (chunk, chunk), 1)

    def relay(t, d):
        x_wait(t, d)

        @pl.when(relay_if(d))
        def _():
            halo_relay(t, d).start()

    apart = row_i ^ col_i

    def inside(h, _):
        hc = cols(h)
        crow = grow[h, 20:21, :]
        for i in range(chunks):
            rows = pl.ds(i * chunk, chunk)
            g = gcol[h, rows, :]
            ccol = g[:, 20:21]
            scores = nt_dot(sq[rows, hc], sk[0 : (i + 1) * chunk, hc])
            parts = []
            for j in range(i + 1):
                s = scores[:, j * chunk : (j + 1) * chunk]
                gap = ccol - crow[:, j * chunk : (j + 1) * chunk]
                if j < i:
                    level = (i ^ j).bit_length() + 7
                    m = s * jnp.exp(gap) * g[:, level : level + 1]
                else:
                    gate = jnp.broadcast_to(g[:, 0:1], (chunk, chunk))
                    for level in range(1, 8):
                        gate = jnp.where(apart >= 1 << (level - 1), g[:, level : level + 1], gate)
                    seen = row_i >= col_i
                    m = jnp.where(seen, s * jnp.exp(jnp.where(seen, gap, 0.0)) * gate, 0.0)
                parts.append(m.astype(BF16))
            low = parts[0] if i == 0 else jnp.concatenate(parts, axis=1)
            mixed[h, rows, :] = jnp.dot(
                low, sv[0 : (i + 1) * chunk, hc], preferred_element_type=F32
            )
        return 0

    lax.fori_loop(0, ROW // 2, inside, 0)
    relay(0, 1)
    relay(0, 3)
    lax.fori_loop(ROW // 2, ROW, inside, 0)

    def reaching(h, _):
        hc = cols(h)
        for i in range(chunks):
            rows = pl.ds(i * chunk, chunk)
            g = gcol[h, rows, :]
            qf = sq[rows, hc].astype(F32) * g[:, 22:23]
            near = jnp.where(x == 2, g[:, 11:12], g[:, 10:11])
            for m, gate in enumerate((g[:, 12:13], g[:, 13:14], g[:, 14:15], near, g[:, 11:12])):
                reached[h, rows, m * hd : (m + 1) * hd] = (qf * gate).astype(BF16)
            v = sg[rows, hc].astype(F32)
            gated[rows, hc] = v / (1.0 + jnp.exp(-v))
        return 0

    for d in range(1, ROW):
        p = (x + ROW - d) % ROW
        for i, (src, dst) in enumerate(((ssend, srecv), (tsend, trecv))):
            pltpu.make_async_remote_copy(
                src_ref=src.at[p],
                dst_ref=dst.at[p],
                send_sem=s_send.at[i, d - 1],
                recv_sem=s_recv.at[i, d - 1],
                device_id={"ctx": rowdev(d)},
                device_id_type=MESH,
            ).wait_recv()
    tot = [trecv[i] for i in range(ROW)]
    st = [srecv[i].astype(F32) for i in range(ROW)]
    pair = st[0] * jnp.exp(tot[1][0:1]) + st[1]
    row_state = (
        pair * jnp.exp((tot[2] + tot[3])[0:1]) + st[2] * jnp.exp(tot[3][0:1]) + st[3]
    )
    rsend[...] = row_state.astype(BF16)
    trsend[...] = tot[0] + tot[1] + tot[2] + tot[3]
    for d in range(1, zn):

        @pl.when(z + d < zn)
        def _():
            for c in r_copies(d):
                c.start()

    lax.fori_loop(0, ROW, reaching, 0)

    for t, d in ((1, 1), (1, 3), (0, 2), (1, 2)):
        relay(t, d)

    for d in range(1, zn):

        @pl.when(z - d >= 0)
        def _():
            for c in r_copies(d):
                c.wait_recv()

    levels = [jnp.zeros((hd, hd), F32) for _ in range(3)]
    decay = jnp.zeros((8, 128), F32)
    for d in range(1, zn):
        other = z + zn - d
        near2 = (z + zn) // 2 == other // 2
        near4 = (z + zn) // 4 == other // 4
        w = jnp.exp(decay)[0:1]
        held = rrecv[d - 1].astype(F32)
        levels[0] = levels[0] + jnp.where(near2, w, 0.0) * held
        levels[1] = levels[1] + jnp.where(near4 & ~near2, w, 0.0) * held
        levels[2] = levels[2] + jnp.where(near4, 0.0, w) * held
        decay = decay + trrecv[d - 1]
    for d in (0, 1, 3, 2):
        xp = (x + d) % ROW
        before = (
            jnp.where(xp >= 1, tot[0], 0.0)
            + jnp.where(xp >= 2, tot[1], 0.0)
            + jnp.where(xp >= 3, tot[2], 0.0)
        )
        w = jnp.exp(before)[0:1]
        for m in range(3):
            lsend[d, m] = (levels[m] * w).astype(BF16)
        near = jnp.where(xp == 1, st[0], jnp.where(xp == 2, pair, jnp.where(xp == 3, st[2], 0.0)))
        lsend[d, 3] = near.astype(BF16)
        lsend[d, 4] = (pair * jnp.exp(tot[2][0:1])).astype(BF16)
        if d > 0:
            l_copy(0, d).start()

            @pl.when(xp == 3)
            def _():
                l_copy(1, d).start()

    lrecv[x, 0:4] = lsend[0, 0:4]

    @pl.when(x == 3)
    def _():
        lrecv[x, 4] = lsend[0, 4]

    for c in own_in:
        c.wait()

    kappa = math.log2(math.e) / math.sqrt(hd)
    qrows = 256
    absent = jnp.where(z == 0, NEG, 0.0).astype(F32)

    def attend(j):
        def body(i, _):
            first = pl.multiple_of(i * qrows, qrows)
            q = qbuf[j, pl.ds(first, qrows), :]
            logits = []
            for s in range(ROW):
                part = nt_dot(q, kbuf[j + s])
                if s < 3:
                    part = part + jnp.where(j + s < 3, absent, 0.0)
                if s == ROW - 1:
                    r = lax.broadcasted_iota(jnp.int32, (qrows, tok), 0) + first
                    c = lax.broadcasted_iota(jnp.int32, (qrows, tok), 1)
                    part = jnp.where(r >= c, part, NEG)
                logits.append(part)
            top = jnp.maximum(
                jnp.maximum(logits[0], logits[1]), jnp.maximum(logits[2], logits[3])
            )
            top = jnp.max(top, axis=1, keepdims=True)
            weights = [jnp.exp2((part - top) * kappa) for part in logits]
            total = jnp.sum(
                (weights[0] + weights[1]) + (weights[2] + weights[3]), axis=1, keepdims=True
            )
            out = None
            for s in range(ROW):
                term = jnp.dot(
                    weights[s].astype(BF16), vbuf[j + s], preferred_element_type=F32
                )
                out = term if out is None else out + term
            obuf[j, pl.ds(first, qrows), :] = (out / total).astype(BF16)
            return 0

        lax.fori_loop(0, tok // qrows, body, 0)

    def turn(k):
        if k < ROW - 1:
            return jnp.where(ROW - 1 - k > x, ROW - 1 - k, ROW - 2 - k)
        return x

    def step(k):
        j = turn(k)
        done = turn(k - 1) if k > 0 else ROW - 1
        for slot in (2, 1, 0):

            @pl.when((z > 0) & (slot >= j) & (slot < done))
            def _():
                for t in (0, 1):
                    halo_wait(t, slot)

        if k < ROW - 1:
            d = (x + ROW - j) % ROW
            x_wait(2, d)
        attend(j)
        if k < ROW - 1:
            o_copy(j).start()
        else:
            o_local(j).start()

    step(0)

    step(1)

    for d in range(1, ROW):
        p = (x + ROW - d) % ROW
        pltpu.make_async_remote_copy(
            src_ref=lsend.at[d, pl.ds(0, 4)],
            dst_ref=lrecv.at[p, pl.ds(0, 4)],
            send_sem=l_send.at[0, d - 1],
            recv_sem=l_recv.at[0, d - 1],
            device_id={"ctx": rowdev(d)},
            device_id_type=MESH,
        ).wait_recv()

        @pl.when(x == 3)
        def _():
            pltpu.make_async_remote_copy(
                src_ref=lsend.at[d, pl.ds(4, 1)],
                dst_ref=lrecv.at[p, pl.ds(4, 1)],
                send_sem=l_send.at[1, d - 1],
                recv_sem=l_recv.at[1, d - 1],
                device_id={"ctx": rowdev(d)},
                device_id_type=MESH,
            ).wait_recv()

    def across(h, acc):
        hc = cols(h)
        squares = []
        states = lrecv[h].reshape(5 * hd, hd)
        for i in range(chunks):
            rows = pl.ds(i * chunk, chunk)
            far = jnp.dot(reached[h, rows, :], states, preferred_element_type=F32)
            out = (mixed[h, rows, :] + far) * gated[rows, hc]
            gated[rows, hc] = out
            squares.append(out * out)
        return tuple(a + s for a, s in zip(acc, squares))

    acc = lax.fori_loop(
        0, ROW, across, tuple(jnp.zeros((chunk, hd), F32) for _ in range(chunks))
    )
    nsend[...] = jnp.zeros_like(nsend)
    for i in range(chunks):
        nsend[i : i + 1, :] = jnp.sum(acc[i].T, axis=0, keepdims=True)
    for d in range(1, hn):
        n_copy(d).start()

    step(2)
    step(3)

    total = nsend[...]
    for d in range(1, hn):
        n_copy(d).wait_recv()
        total = total + nrecv[d - 1]
    scale = lax.rsqrt(total / (hn * ROW * hd) + 1e-05)
    for i in range(chunks):
        rows = pl.ds(i * chunk, chunk)
        scale_col = jnp.broadcast_to(scale[i : i + 1], (chunk, chunk)).T
        for h in range(ROW):
            hs = slice(h * hd, (h + 1) * hd)
            mout[rows, hs] = (gated[rows, hs] * scale_col * gain_ref[:, hs]).astype(BF16)
    mix_out = pltpu.make_async_copy(mout, mo_hbm, out_sem.at[0])
    mix_out.start()

    for d in range(1, ROW):
        for t in range(3):
            x_copy(t, d).wait_send()
        for c in s_copies(d):
            c.wait_send()
        l_copy(0, d).wait_send()

        @pl.when((x + d) % ROW == 3)
        def _():
            l_copy(1, d).wait_send()

        @pl.when(relay_if(d))
        def _():
            for t in (0, 1):
                halo_relay(t, d).wait_send()

    @pl.when(own_halo)
    def _():
        for t in (0, 1):
            halo_own(t).wait_send()

    for d in range(1, zn):

        @pl.when(z + d < zn)
        def _():
            for c in r_copies(d):
                c.wait_send()

    for d in range(1, hn):
        n_copy(d).wait_send()
    for j in range(ROW):

        @pl.when(x != j)
        def _():
            o_copy(j).wait_send()
            pltpu.make_async_remote_copy(
                src_ref=obuf.at[j],
                dst_ref=ao_hbm.at[:, cols(j)],
                send_sem=o_send.at[j],
                recv_sem=o_recv.at[j],
                device_id={"ctx": z * ROW + j},
                device_id_type=MESH,
            ).wait_recv()

        @pl.when(x == j)
        def _():
            o_local(j).wait()

    mix_out.wait()


def hbm(*arrays):
    return [pltpu.with_memory_space_constraint(a, pltpu.HBM) for a in arrays]


def shards(zn, hn, sq, sk, sv, sg, ld, lg, gain, aq, ak, av):
    tok = sq.shape[0]
    heads = ld.shape[0]
    hd = sq.shape[1] // heads
    wide = heads * hd
    dma = pltpu.SemaphoreType.DMA
    vm = pltpu.VMEM
    anywhere = pl.BlockSpec(memory_space=pltpu.HBM)
    here = pl.BlockSpec(memory_space=pltpu.VMEM)
    out = jax.ShapeDtypeStruct((tok, wide), BF16)
    return pl.pallas_call(
        functools.partial(kernel, zn, hn),
        out_shape=(out, out),
        in_specs=[anywhere] * 4 + [here, anywhere, here] + [anywhere] * 3,
        out_specs=(anywhere, anywhere),
        scratch_shapes=[
            vm((tok, wide), BF16),
            vm((tok, wide), BF16),
            vm((tok, wide), BF16),
            vm((tok, wide), BF16),
            vm((4, tok, hd), BF16),
            vm((7, tok, hd), BF16),
            vm((7, tok, hd), BF16),
            vm((4, tok, hd), BF16),
            vm((lg.shape[1], heads, tok), F32),
            vm((heads, 32, tok), F32),
            vm((heads, tok, 32), F32),
            vm((heads, tok, hd), F32),
            vm((tok, wide), F32),
            vm((heads, tok, 5 * hd), BF16),
            vm((tok, wide), BF16),
            vm((4, hd, hd), BF16),
            vm((4, hd, hd), BF16),
            vm((4, 8, 128), F32),
            vm((4, 8, 128), F32),
            vm((hd, hd), BF16),
            vm((max(zn - 1, 1), hd, hd), BF16),
            vm((8, 128), F32),
            vm((max(zn - 1, 1), 8, 128), F32),
            vm((4, 5, hd, hd), BF16),
            vm((4, 5, hd, hd), BF16),
            vm((8, 128), F32),
            vm((max(hn - 1, 1), 8, 128), F32),
            dma((8,)),
            dma((3, 3)),
            dma((3, 3)),
            dma((2, 4)),
            dma((2, 4)),
            dma((2, 3)),
            dma((2, 3)),
            dma((2, max(zn - 1, 1))),
            dma((2, max(zn - 1, 1))),
            dma((2, 3)),
            dma((2, 3)),
            dma((max(hn - 1, 1),)),
            dma((max(hn - 1, 1),)),
            dma((4,)),
            dma((4,)),
            dma((2,)),
        ],
        compiler_params=pltpu.CompilerParams(
            collective_id=0, has_side_effects=True, vmem_limit_bytes=48 * 1024 * 1024
        ),
        cost_estimate=pl.CostEstimate(
            flops=3_000_000_000, bytes_accessed=5_000_000, transcendentals=5_000_000
        ),
    )(*hbm(sq, sk, sv, sg), ld, *hbm(jnp.transpose(lg, (1, 0, 2))), gain.reshape(1, wide), *hbm(aq, ak, av))


def solution(mesh):
    zn = mesh.shape["ctx"] // ROW
    hn = mesh.shape["head"]
    return jax.shard_map(
        functools.partial(shards, zn, hn),
        mesh=mesh,
        in_specs=(
            P("ctx", "head"),
            P("ctx", "head"),
            P("ctx", "head"),
            P("ctx", "head"),
            P("head", "ctx"),
            P("head", None, "ctx"),
            P("head"),
            P("ctx", "head"),
            P("ctx", "head"),
            P("ctx", "head"),
        ),
        out_specs=(P("ctx", "head"), P("ctx", "head")),
        check_vma=False,
    )
```

```python
import functools
import math

import jax
import jax.numpy as jnp
from jax import lax
from jax.experimental import pallas as pl
from jax.experimental.pallas import tpu as pltpu
from jax.sharding import PartitionSpec as P

MESH = pl.DeviceIdType.MESH
ROW = 4
F32 = jnp.float32
BF16 = jnp.bfloat16
NEG = -1e30


def nt_dot(a, b):
    return lax.dot_general(a, b, (((1,), (1,)), ((), ())), preferred_element_type=F32)


def tn_dot(a, b):
    return lax.dot_general(a, b, (((0,), (0,)), ((), ())), preferred_element_type=F32)


def kernel(
    zn,
    hn,
    sq_hbm,
    sk_hbm,
    sv_hbm,
    sg_hbm,
    ld_hbm,
    lg_hbm,
    gain_hbm,
    aq_hbm,
    ak_hbm,
    av_hbm,
    mo_hbm,
    ao_hbm,
    sq,
    sk,
    sv,
    sg,
    qbuf,
    kbuf,
    vbuf,
    obuf,
    lgbuf,
    ldbuf,
    gainbuf,
    grow,
    gcol,
    mixed,
    gated,
    reached,
    mout,
    ssend,
    srecv,
    tsend,
    trecv,
    rsend,
    rrecv,
    trsend,
    trrecv,
    lsend,
    lrecv,
    nsend,
    nrecv,
    loc_sem,
    x_send,
    x_recv,
    h_send,
    h_recv,
    s_send,
    s_recv,
    r_send,
    r_recv,
    l_send,
    l_recv,
    n_send,
    n_recv,
    o_send,
    o_recv,
    out_sem,
    ready,
):
    me = lax.axis_index("ctx")
    mh = lax.axis_index("head")
    z = me // ROW
    x = me % ROW
    tok = qbuf.shape[1]
    hd = qbuf.shape[2]
    chunk = 128
    chunks = tok // chunk

    def rowdev(d):
        return z * ROW + (x + d) % ROW

    def cols(h):
        return pl.ds(pl.multiple_of(h * hd, hd), hd)

    rrecv[...] = jnp.zeros_like(rrecv)
    trrecv[...] = jnp.zeros_like(trrecv)

    @pl.when(x != 3)
    def _():
        lrecv[:, 4] = jnp.zeros_like(lrecv[:, 4])

    @pl.when(z == 0)
    def _():
        kbuf[0:3] = jnp.zeros((3, tok, hd), BF16)
        vbuf[0:3] = jnp.zeros((3, tok, hd), BF16)

    barrier = pltpu.get_barrier_semaphore()
    for d in range(1, ROW):
        pl.semaphore_signal(barrier, inc=1, device_id={"ctx": rowdev(d)}, device_id_type=MESH)
    for d in range(1, zn):

        @pl.when(z + d < zn)
        def _():
            pl.semaphore_signal(
                barrier, inc=1, device_id={"ctx": (z + d) * ROW + x}, device_id_type=MESH
            )

    for d in range(1, hn):
        pl.semaphore_signal(barrier, inc=1, device_id={"head": (mh + d) % hn}, device_id_type=MESH)

    state_in = [
        pltpu.make_async_copy(src, dst, loc_sem.at[i])
        for i, (src, dst) in enumerate(((sk_hbm, sk), (sv_hbm, sv), (sq_hbm, sq), (sg_hbm, sg)))
    ]
    gates_in = pltpu.make_async_copy(lg_hbm, lgbuf, loc_sem.at[7])
    decay_in = pltpu.make_async_copy(ld_hbm, ldbuf, loc_sem.at[8])
    gain_in = pltpu.make_async_copy(gain_hbm, gainbuf, loc_sem.at[9])
    decay_in.start()
    gates_in.start()
    for c in state_in:
        c.start()
    gain_in.start()
    att = ((ak_hbm, kbuf, 3), (av_hbm, vbuf, 3), (aq_hbm, qbuf, 0))
    own_in = [
        pltpu.make_async_copy(src.at[:, cols(x)], dst.at[base + x], loc_sem.at[4 + i])
        for i, (src, dst, base) in enumerate(att)
    ]
    for c in own_in:
        c.start()

    def x_copy(t, d):
        src, dst, base = att[t]
        return pltpu.make_async_remote_copy(
            src_ref=src.at[:, cols((x + d) % ROW)],
            dst_ref=dst.at[base + x],
            send_sem=x_send.at[t, d - 1],
            recv_sem=x_recv.at[t, d - 1],
            device_id={"ctx": rowdev(d)},
            device_id_type=MESH,
        )

    def x_wait(t, d):
        src, dst, base = att[t]
        pltpu.make_async_remote_copy(
            src_ref=src.at[:, cols((x + d) % ROW)],
            dst_ref=dst.at[base + (x + ROW - d) % ROW],
            send_sem=x_send.at[t, d - 1],
            recv_sem=x_recv.at[t, d - 1],
            device_id={"ctx": rowdev(d)},
            device_id_type=MESH,
        ).wait_recv()

    def halo_own(t):
        src, dst, _ = att[t]
        return pltpu.make_async_remote_copy(
            src_ref=src.at[:, cols(x)],
            dst_ref=dst.at[(x + ROW - 1) % ROW],
            send_sem=h_send.at[t, 0],
            recv_sem=h_recv.at[t, (x + ROW - 1) % ROW],
            device_id={"ctx": me + ROW},
            device_id_type=MESH,
        )

    def halo_relay(t, d):
        dst = att[t][1]
        block = (x + ROW - d) % ROW
        return pltpu.make_async_remote_copy(
            src_ref=dst.at[3 + block],
            dst_ref=dst.at[(block + ROW - 1) % ROW],
            send_sem=h_send.at[t, d],
            recv_sem=h_recv.at[t, (block + ROW - 1) % ROW],
            device_id={"ctx": me + ROW},
            device_id_type=MESH,
        )

    def relay_if(d):
        return ((x + ROW - d) % ROW >= 1) & (z < zn - 1)

    def halo_wait(t, slot):
        dst = att[t][1]
        pltpu.make_async_remote_copy(
            src_ref=dst.at[slot],
            dst_ref=dst.at[slot],
            send_sem=h_send.at[t, 0],
            recv_sem=h_recv.at[t, slot],
            device_id={"ctx": (me + ROW) % (zn * ROW)},
            device_id_type=MESH,
        ).wait_recv()

    def s_copies(d):
        p = (x + d) % ROW
        return [
            pltpu.make_async_remote_copy(
                src_ref=src.at[p],
                dst_ref=dst.at[x],
                send_sem=s_send.at[i, d - 1],
                recv_sem=s_recv.at[i, d - 1],
                device_id={"ctx": rowdev(d)},
                device_id_type=MESH,
            )
            for i, (src, dst) in enumerate(((ssend, srecv), (tsend, trecv)))
        ]

    def r_copies(d):
        return [
            pltpu.make_async_remote_copy(
                src_ref=src,
                dst_ref=dst.at[d - 1],
                send_sem=r_send.at[i, d - 1],
                recv_sem=r_recv.at[i, d - 1],
                device_id={"ctx": ((z + d) % zn) * ROW + x},
                device_id_type=MESH,
            )
            for i, (src, dst) in enumerate(((rsend, rrecv), (trsend, trrecv)))
        ]

    def l_copy(i, d):
        part = pl.ds(0, 4) if i == 0 else pl.ds(4, 1)
        return pltpu.make_async_remote_copy(
            src_ref=lsend.at[d, part],
            dst_ref=lrecv.at[x, part],
            send_sem=l_send.at[i, d - 1],
            recv_sem=l_recv.at[i, d - 1],
            device_id={"ctx": rowdev(d)},
            device_id_type=MESH,
        )

    def n_copy(d):
        return pltpu.make_async_remote_copy(
            src_ref=nsend,
            dst_ref=nrecv.at[d - 1],
            send_sem=n_send.at[d - 1],
            recv_sem=n_recv.at[d - 1],
            device_id={"head": (mh + d) % hn},
            device_id_type=MESH,
        )

    def o_copy(j):
        return pltpu.make_async_remote_copy(
            src_ref=obuf.at[j],
            dst_ref=ao_hbm.at[:, cols(x)],
            send_sem=o_send.at[j],
            recv_sem=o_recv.at[x],
            device_id={"ctx": z * ROW + j},
            device_id_type=MESH,
        )

    def o_local(j):
        return pltpu.make_async_copy(obuf.at[j], ao_hbm.at[:, cols(x)], out_sem.at[1])

    pl.semaphore_wait(barrier, ROW - 1 + z + hn - 1)
    for d in range(1, zn):

        @pl.when(z - d >= 0)
        def _():
            pl.semaphore_signal(
                ready.at[d - 1], inc=1, device_id={"ctx": (z - d) * ROW + x}, device_id_type=MESH
            )

    for d in (1, 3):
        x_copy(0, d).start()

    decay_in.wait()
    lane = lax.broadcasted_iota(jnp.int32, (8, tok), 1)
    cum = jnp.concatenate([ldbuf[...], jnp.zeros((8 - ROW, tok), F32)], axis=0)
    shift = 1
    while shift < tok:
        cum = cum + jnp.where(lane >= shift, pltpu.roll(cum, shift, axis=1), 0.0)
        shift *= 2
    last = cum[:, tok - 1 : tok]
    tail = jnp.exp(last - cum)
    reach = jnp.exp(cum)
    gates_in.wait()
    for h in range(ROW):
        grow[h, 0:20, :] = lgbuf[:, h, :]
        grow[h, 20:21, :] = cum[h : h + 1]
        grow[h, 21:22, :] = tail[h : h + 1]
        grow[h, 22:23, :] = reach[h : h + 1]
        grow[h, 23:24, :] = cum[h : h + 1]
        grow[h, 24:32, :] = cum
        tsend[h] = jnp.broadcast_to(last[h : h + 1], (8, 128))
        gcol[h] = grow[h].T

    state_in[0].wait()
    state_in[1].wait()

    def summary(h, _):
        kf = sk[:, cols(h)].astype(F32)
        low = (kf * gcol[h, :, 21:22]).astype(BF16)
        ssend[h] = tn_dot(low, sv[:, cols(h)]).astype(BF16)
        return 0

    lax.fori_loop(0, ROW, summary, 0)
    for d in (1, 3, 2):
        for c in s_copies(d):
            c.start()
    for t, d in ((1, 1), (1, 3), (0, 2), (1, 2), (2, 1), (2, 3), (2, 2)):
        x_copy(t, d).start()
    own_halo = (x >= 1) & (z < zn - 1)

    @pl.when(z < zn - 1)
    def _():
        pl.semaphore_wait(ready.at[0], 1)

    @pl.when(own_halo)
    def _():
        halo_own(0).start()
        halo_own(1).start()

    srecv[x] = ssend[x]
    trecv[x] = tsend[x]

    state_in[2].wait()
    state_in[3].wait()
    row_i = lax.broadcasted_iota(jnp.int32, (chunk, chunk), 0)
    col_i = lax.broadcasted_iota(jnp.int32, (chunk, chunk), 1)

    def relay(t, d):
        x_wait(t, d)

        @pl.when(relay_if(d))
        def _():
            halo_relay(t, d).start()

    apart = row_i ^ col_i

    def inside(h, _):
        hc = cols(h)
        crow = grow[h, 20:21, :]
        for i in range(chunks):
            rows = pl.ds(i * chunk, chunk)
            g = gcol[h, rows, :]
            ccol = g[:, 20:21]
            scores = nt_dot(sq[rows, hc], sk[0 : (i + 1) * chunk, hc])
            parts = []
            for j in range(i + 1):
                s = scores[:, j * chunk : (j + 1) * chunk]
                gap = ccol - crow[:, j * chunk : (j + 1) * chunk]
                if j < i:
                    level = (i ^ j).bit_length() + 7
                    m = s * jnp.exp(gap) * g[:, level : level + 1]
                else:
                    gate = jnp.broadcast_to(g[:, 0:1], (chunk, chunk))
                    for level in range(1, 8):
                        gate = jnp.where(apart >= 1 << (level - 1), g[:, level : level + 1], gate)
                    seen = row_i >= col_i
                    m = jnp.where(seen, s * jnp.exp(jnp.where(seen, gap, 0.0)) * gate, 0.0)
                parts.append(m.astype(BF16))
            low = parts[0] if i == 0 else jnp.concatenate(parts, axis=1)
            mixed[h, rows, :] = jnp.dot(
                low, sv[0 : (i + 1) * chunk, hc], preferred_element_type=F32
            )
        return 0

    lax.fori_loop(0, ROW // 2, inside, 0)
    relay(0, 1)
    relay(0, 3)
    lax.fori_loop(ROW // 2, ROW, inside, 0)

    def reaching(h, _):
        hc = cols(h)
        for i in range(chunks):
            rows = pl.ds(i * chunk, chunk)
            g = gcol[h, rows, :]
            qf = sq[rows, hc].astype(F32) * g[:, 22:23]
            near = jnp.where(x == 2, g[:, 11:12], g[:, 10:11])
            for m, gate in enumerate((g[:, 12:13], g[:, 13:14], g[:, 14:15], near, g[:, 11:12])):
                reached[h, rows, m * hd : (m + 1) * hd] = (qf * gate).astype(BF16)
            v = sg[rows, hc].astype(F32)
            gated[rows, hc] = v / (1.0 + jnp.exp(-v))
        return 0

    for d in range(1, ROW):
        p = (x + ROW - d) % ROW
        for i, (src, dst) in enumerate(((ssend, srecv), (tsend, trecv))):
            pltpu.make_async_remote_copy(
                src_ref=src.at[p],
                dst_ref=dst.at[p],
                send_sem=s_send.at[i, d - 1],
                recv_sem=s_recv.at[i, d - 1],
                device_id={"ctx": rowdev(d)},
                device_id_type=MESH,
            ).wait_recv()
    tot = [trecv[i] for i in range(ROW)]
    st = [srecv[i].astype(F32) for i in range(ROW)]
    pair = st[0] * jnp.exp(tot[1][0:1]) + st[1]
    row_state = (
        pair * jnp.exp((tot[2] + tot[3])[0:1]) + st[2] * jnp.exp(tot[3][0:1]) + st[3]
    )
    rsend[...] = row_state.astype(BF16)
    trsend[...] = tot[0] + tot[1] + tot[2] + tot[3]
    for d in range(1, zn):

        @pl.when(z + d < zn)
        def _():
            if d > 1:
                pl.semaphore_wait(ready.at[d - 1], 1)
            for c in r_copies(d):
                c.start()

    lax.fori_loop(0, ROW, reaching, 0)

    for t, d in ((1, 1), (1, 3), (0, 2), (1, 2)):
        relay(t, d)

    for d in range(1, zn):

        @pl.when(z - d >= 0)
        def _():
            for c in r_copies(d):
                c.wait_recv()

    levels = [jnp.zeros((hd, hd), F32) for _ in range(3)]
    decay = jnp.zeros((8, 128), F32)
    for d in range(1, zn):
        other = z + zn - d
        near2 = (z + zn) // 2 == other // 2
        near4 = (z + zn) // 4 == other // 4
        w = jnp.exp(decay)[0:1]
        held = rrecv[d - 1].astype(F32)
        levels[0] = levels[0] + jnp.where(near2, w, 0.0) * held
        levels[1] = levels[1] + jnp.where(near4 & ~near2, w, 0.0) * held
        levels[2] = levels[2] + jnp.where(near4, 0.0, w) * held
        decay = decay + trrecv[d - 1]
    for d in (0, 1, 3, 2):
        xp = (x + d) % ROW
        before = (
            jnp.where(xp >= 1, tot[0], 0.0)
            + jnp.where(xp >= 2, tot[1], 0.0)
            + jnp.where(xp >= 3, tot[2], 0.0)
        )
        w = jnp.exp(before)[0:1]
        for m in range(3):
            lsend[d, m] = (levels[m] * w).astype(BF16)
        near = jnp.where(xp == 1, st[0], jnp.where(xp == 2, pair, jnp.where(xp == 3, st[2], 0.0)))
        lsend[d, 3] = near.astype(BF16)
        lsend[d, 4] = (pair * jnp.exp(tot[2][0:1])).astype(BF16)
        if d > 0:
            l_copy(0, d).start()

            @pl.when(xp == 3)
            def _():
                l_copy(1, d).start()

    lrecv[x, 0:4] = lsend[0, 0:4]

    @pl.when(x == 3)
    def _():
        lrecv[x, 4] = lsend[0, 4]

    for c in own_in:
        c.wait()

    kappa = math.log2(math.e) / math.sqrt(hd)
    qrows = 256
    absent = jnp.where(z == 0, NEG, 0.0).astype(F32)

    def attend(j):
        def body(i, _):
            first = pl.multiple_of(i * qrows, qrows)
            q = qbuf[j, pl.ds(first, qrows), :]
            logits = []
            for s in range(ROW):
                part = nt_dot(q, kbuf[j + s])
                if s < 3:
                    part = part + jnp.where(j + s < 3, absent, 0.0)
                if s == ROW - 1:
                    r = lax.broadcasted_iota(jnp.int32, (qrows, tok), 0) + first
                    c = lax.broadcasted_iota(jnp.int32, (qrows, tok), 1)
                    part = jnp.where(r >= c, part, NEG)
                logits.append(part)
            top = jnp.maximum(
                jnp.maximum(logits[0], logits[1]), jnp.maximum(logits[2], logits[3])
            )
            top = jnp.max(top, axis=1, keepdims=True)
            weights = [jnp.exp2((part - top) * kappa) for part in logits]
            total = jnp.sum(
                (weights[0] + weights[1]) + (weights[2] + weights[3]), axis=1, keepdims=True
            )
            out = None
            for s in range(ROW):
                term = jnp.dot(
                    weights[s].astype(BF16), vbuf[j + s], preferred_element_type=F32
                )
                out = term if out is None else out + term
            obuf[j, pl.ds(first, qrows), :] = (out / total).astype(BF16)
            return 0

        lax.fori_loop(0, tok // qrows, body, 0)

    turns = (ROW - 1 - x, (x + 2) % ROW, x + 1 - 2 * (x % 2), x)

    def step(k):
        j = turns[k]
        done = ROW - 1
        for earlier in turns[:k]:
            done = jnp.minimum(done, earlier)
        for slot in (2, 1, 0):

            @pl.when((z > 0) & (slot >= j) & (slot < done))
            def _():
                for t in (0, 1):
                    halo_wait(t, slot)

        if k < ROW - 1:
            d = (x + ROW - j) % ROW
            x_wait(2, d)
        attend(j)
        if k < ROW - 1:
            o_copy(j).start()
        else:
            o_local(j).start()

    step(0)

    step(1)

    step(2)

    for d in range(1, ROW):
        p = (x + ROW - d) % ROW
        pltpu.make_async_remote_copy(
            src_ref=lsend.at[d, pl.ds(0, 4)],
            dst_ref=lrecv.at[p, pl.ds(0, 4)],
            send_sem=l_send.at[0, d - 1],
            recv_sem=l_recv.at[0, d - 1],
            device_id={"ctx": rowdev(d)},
            device_id_type=MESH,
        ).wait_recv()

        @pl.when(x == 3)
        def _():
            pltpu.make_async_remote_copy(
                src_ref=lsend.at[d, pl.ds(4, 1)],
                dst_ref=lrecv.at[p, pl.ds(4, 1)],
                send_sem=l_send.at[1, d - 1],
                recv_sem=l_recv.at[1, d - 1],
                device_id={"ctx": rowdev(d)},
                device_id_type=MESH,
            ).wait_recv()

    def across(h, acc):
        hc = cols(h)
        squares = []
        states = lrecv[h].reshape(5 * hd, hd)
        for i in range(chunks):
            rows = pl.ds(i * chunk, chunk)
            far = jnp.dot(reached[h, rows, :], states, preferred_element_type=F32)
            out = (mixed[h, rows, :] + far) * gated[rows, hc]
            gated[rows, hc] = out
            squares.append(out * out)
        return tuple(a + s for a, s in zip(acc, squares))

    acc = lax.fori_loop(
        0, ROW, across, tuple(jnp.zeros((chunk, hd), F32) for _ in range(chunks))
    )
    nsend[...] = jnp.zeros_like(nsend)
    for i in range(chunks):
        nsend[i : i + 1, :] = jnp.sum(acc[i].T, axis=0, keepdims=True)
    for d in range(1, hn):
        n_copy(d).start()

    step(3)

    total = nsend[...]
    for d in range(1, hn):
        n_copy(d).wait_recv()
        total = total + nrecv[d - 1]
    gain_in.wait()
    scale = lax.rsqrt(total / (hn * ROW * hd) + 1e-05)
    for i in range(chunks):
        rows = pl.ds(i * chunk, chunk)
        scale_col = jnp.broadcast_to(scale[i : i + 1], (chunk, chunk)).T
        for h in range(ROW):
            hs = slice(h * hd, (h + 1) * hd)
            mout[rows, hs] = (gated[rows, hs] * scale_col * gainbuf[:, hs]).astype(BF16)
    mix_out = pltpu.make_async_copy(mout, mo_hbm, out_sem.at[0])
    mix_out.start()

    for d in range(1, ROW):
        for t in range(3):
            x_copy(t, d).wait_send()
        for c in s_copies(d):
            c.wait_send()
        l_copy(0, d).wait_send()

        @pl.when((x + d) % ROW == 3)
        def _():
            l_copy(1, d).wait_send()

        @pl.when(relay_if(d))
        def _():
            for t in (0, 1):
                halo_relay(t, d).wait_send()

    @pl.when(own_halo)
    def _():
        for t in (0, 1):
            halo_own(t).wait_send()

    for d in range(1, zn):

        @pl.when(z + d < zn)
        def _():
            for c in r_copies(d):
                c.wait_send()

    for d in range(1, hn):
        n_copy(d).wait_send()
    for j in range(ROW):

        @pl.when(x != j)
        def _():
            o_copy(j).wait_send()
            pltpu.make_async_remote_copy(
                src_ref=obuf.at[j],
                dst_ref=ao_hbm.at[:, cols(j)],
                send_sem=o_send.at[j],
                recv_sem=o_recv.at[j],
                device_id={"ctx": z * ROW + j},
                device_id_type=MESH,
            ).wait_recv()

        @pl.when(x == j)
        def _():
            o_local(j).wait()

    mix_out.wait()


def hbm(*arrays):
    return [pltpu.with_memory_space_constraint(a, pltpu.HBM) for a in arrays]


def shards(zn, hn, sq, sk, sv, sg, ld, lg, gain, aq, ak, av):
    tok = sq.shape[0]
    heads = ld.shape[0]
    hd = sq.shape[1] // heads
    wide = heads * hd
    dma = pltpu.SemaphoreType.DMA
    vm = pltpu.VMEM
    anywhere = pl.BlockSpec(memory_space=pltpu.HBM)
    out = jax.ShapeDtypeStruct((tok, wide), BF16)
    return pl.pallas_call(
        functools.partial(kernel, zn, hn),
        out_shape=(out, out),
        in_specs=[anywhere] * 10,
        out_specs=(anywhere, anywhere),
        scratch_shapes=[
            vm((tok, wide), BF16),
            vm((tok, wide), BF16),
            vm((tok, wide), BF16),
            vm((tok, wide), BF16),
            vm((4, tok, hd), BF16),
            vm((7, tok, hd), BF16),
            vm((7, tok, hd), BF16),
            vm((4, tok, hd), BF16),
            vm((lg.shape[1], heads, tok), F32),
            vm((heads, tok), F32),
            vm((1, wide), F32),
            vm((heads, 32, tok), F32),
            vm((heads, tok, 32), F32),
            vm((heads, tok, hd), F32),
            vm((tok, wide), F32),
            vm((heads, tok, 5 * hd), BF16),
            vm((tok, wide), BF16),
            vm((4, hd, hd), BF16),
            vm((4, hd, hd), BF16),
            vm((4, 8, 128), F32),
            vm((4, 8, 128), F32),
            vm((hd, hd), BF16),
            vm((max(zn - 1, 1), hd, hd), BF16),
            vm((8, 128), F32),
            vm((max(zn - 1, 1), 8, 128), F32),
            vm((4, 5, hd, hd), BF16),
            vm((4, 5, hd, hd), BF16),
            vm((8, 128), F32),
            vm((max(hn - 1, 1), 8, 128), F32),
            dma((10,)),
            dma((3, 3)),
            dma((3, 3)),
            dma((2, 4)),
            dma((2, 4)),
            dma((2, 3)),
            dma((2, 3)),
            dma((2, max(zn - 1, 1))),
            dma((2, max(zn - 1, 1))),
            dma((2, 3)),
            dma((2, 3)),
            dma((max(hn - 1, 1),)),
            dma((max(hn - 1, 1),)),
            dma((4,)),
            dma((4,)),
            dma((2,)),
            pltpu.SemaphoreType.REGULAR((max(zn - 1, 1),)),
        ],
        compiler_params=pltpu.CompilerParams(
            collective_id=0, has_side_effects=True, vmem_limit_bytes=48 * 1024 * 1024
        ),
        cost_estimate=pl.CostEstimate(
            flops=3_000_000_000, bytes_accessed=5_000_000, transcendentals=5_000_000
        ),
    )(*hbm(sq, sk, sv, sg, ld, jnp.transpose(lg, (1, 0, 2)), gain.reshape(1, wide), aq, ak, av))


def solution(mesh):
    zn = mesh.shape["ctx"] // ROW
    hn = mesh.shape["head"]
    return jax.shard_map(
        functools.partial(shards, zn, hn),
        mesh=mesh,
        in_specs=(
            P("ctx", "head"),
            P("ctx", "head"),
            P("ctx", "head"),
            P("ctx", "head"),
            P("head", "ctx"),
            P("head", None, "ctx"),
            P("head"),
            P("ctx", "head"),
            P("ctx", "head"),
            P("ctx", "head"),
        ),
        out_specs=(P("ctx", "head"), P("ctx", "head")),
        check_vma=False,
    )
```

```python
import functools
import math

import jax
import jax.numpy as jnp
from jax import lax
from jax.experimental import pallas as pl
from jax.experimental.pallas import tpu as pltpu
from jax.sharding import PartitionSpec as P

MESH = pl.DeviceIdType.MESH
ROW = 4
F32 = jnp.float32
BF16 = jnp.bfloat16
NEG = -1e30


def nt_dot(a, b):
    return lax.dot_general(a, b, (((1,), (1,)), ((), ())), preferred_element_type=F32)


def tn_dot(a, b):
    return lax.dot_general(a, b, (((0,), (0,)), ((), ())), preferred_element_type=F32)


def kernel(
    zn,
    hn,
    sq_hbm,
    sk_hbm,
    sv_hbm,
    sg_hbm,
    ld_hbm,
    lg_hbm,
    gain_hbm,
    aq_hbm,
    ak_hbm,
    av_hbm,
    mo_hbm,
    ao_hbm,
    sq,
    sk,
    sv,
    sg,
    qbuf,
    kbuf,
    vbuf,
    obuf,
    lgbuf,
    ldbuf,
    gainbuf,
    grow,
    gcol,
    mixed,
    gated,
    reached,
    mout,
    ssend,
    srecv,
    tsend,
    trecv,
    rsend,
    rrecv,
    trsend,
    trrecv,
    asend,
    arecv,
    lsend,
    lrecv,
    nsend,
    nrecv,
    loc_sem,
    x_send,
    x_recv,
    h_send,
    h_recv,
    s_send,
    s_recv,
    r_send,
    r_recv,
    l_send,
    l_recv,
    n_send,
    n_recv,
    o_send,
    o_recv,
    out_sem,
    ready,
    a_send,
    a_recv,
):
    me = lax.axis_index("ctx")
    mh = lax.axis_index("head")
    z = me // ROW
    x = me % ROW
    tok = qbuf.shape[1]
    hd = qbuf.shape[2]
    chunk = 128
    chunks = tok // chunk

    def rowdev(d):
        return z * ROW + (x + d) % ROW

    def cols(h):
        return pl.ds(pl.multiple_of(h * hd, hd), hd)

    zl = z % 4

    def sends_to(d):
        return ((zl + d < 4) | (z == 3)) & (z + d < zn)

    def hears_from(d):
        return (zl >= d) | (z - d == 3)

    reaches = range(1, min(zn, 5))
    group = range(1, min(zn, 4))

    rrecv[...] = jnp.zeros_like(rrecv)
    arecv[...] = jnp.zeros_like(arecv)
    trrecv[...] = jnp.zeros_like(trrecv)

    lrecv[...] = jnp.zeros_like(lrecv)

    @pl.when(z == 0)
    def _():
        kbuf[0:3] = jnp.zeros((3, tok, hd), BF16)
        vbuf[0:3] = jnp.zeros((3, tok, hd), BF16)

    barrier = pltpu.get_barrier_semaphore()
    for d in range(1, ROW):
        pl.semaphore_signal(barrier, inc=1, device_id={"ctx": rowdev(d)}, device_id_type=MESH)
    for d in reaches:

        @pl.when(sends_to(d))
        def _():
            pl.semaphore_signal(
                barrier, inc=1, device_id={"ctx": (z + d) * ROW + x}, device_id_type=MESH
            )

    for d in range(1, hn):
        pl.semaphore_signal(barrier, inc=1, device_id={"head": (mh + d) % hn}, device_id_type=MESH)

    state_in = [
        pltpu.make_async_copy(src, dst, loc_sem.at[i])
        for i, (src, dst) in enumerate(((sk_hbm, sk), (sv_hbm, sv), (sq_hbm, sq), (sg_hbm, sg)))
    ]
    gates_in = pltpu.make_async_copy(lg_hbm, lgbuf, loc_sem.at[7])
    decay_in = pltpu.make_async_copy(ld_hbm, ldbuf, loc_sem.at[8])
    gain_in = pltpu.make_async_copy(gain_hbm, gainbuf, loc_sem.at[9])
    decay_in.start()
    gates_in.start()
    for c in state_in:
        c.start()
    gain_in.start()
    att = ((ak_hbm, kbuf, 3), (av_hbm, vbuf, 3), (aq_hbm, qbuf, 0))
    own_in = [
        pltpu.make_async_copy(src.at[:, cols(x)], dst.at[base + x], loc_sem.at[4 + i])
        for i, (src, dst, base) in enumerate(att)
    ]
    for c in own_in:
        c.start()

    def x_copy(t, d):
        src, dst, base = att[t]
        return pltpu.make_async_remote_copy(
            src_ref=src.at[:, cols((x + d) % ROW)],
            dst_ref=dst.at[base + x],
            send_sem=x_send.at[t, d - 1],
            recv_sem=x_recv.at[t, d - 1],
            device_id={"ctx": rowdev(d)},
            device_id_type=MESH,
        )

    def x_wait(t, d):
        src, dst, base = att[t]
        pltpu.make_async_remote_copy(
            src_ref=src.at[:, cols((x + d) % ROW)],
            dst_ref=dst.at[base + (x + ROW - d) % ROW],
            send_sem=x_send.at[t, d - 1],
            recv_sem=x_recv.at[t, d - 1],
            device_id={"ctx": rowdev(d)},
            device_id_type=MESH,
        ).wait_recv()

    def halo_own(t):
        src, dst, _ = att[t]
        return pltpu.make_async_remote_copy(
            src_ref=src.at[:, cols(x)],
            dst_ref=dst.at[(x + ROW - 1) % ROW],
            send_sem=h_send.at[t, 0],
            recv_sem=h_recv.at[t, (x + ROW - 1) % ROW],
            device_id={"ctx": me + ROW},
            device_id_type=MESH,
        )

    def halo_relay(t, d):
        dst = att[t][1]
        block = (x + ROW - d) % ROW
        return pltpu.make_async_remote_copy(
            src_ref=dst.at[3 + block],
            dst_ref=dst.at[(block + ROW - 1) % ROW],
            send_sem=h_send.at[t, d],
            recv_sem=h_recv.at[t, (block + ROW - 1) % ROW],
            device_id={"ctx": me + ROW},
            device_id_type=MESH,
        )

    def relay_if(d):
        return ((x + ROW - d) % ROW >= 1) & (z < zn - 1)

    def halo_wait(t, slot):
        dst = att[t][1]
        pltpu.make_async_remote_copy(
            src_ref=dst.at[slot],
            dst_ref=dst.at[slot],
            send_sem=h_send.at[t, 0],
            recv_sem=h_recv.at[t, slot],
            device_id={"ctx": (me + ROW) % (zn * ROW)},
            device_id_type=MESH,
        ).wait_recv()

    def s_copies(d):
        p = (x + d) % ROW
        return [
            pltpu.make_async_remote_copy(
                src_ref=src.at[p],
                dst_ref=dst.at[x],
                send_sem=s_send.at[i, d - 1],
                recv_sem=s_recv.at[i, d - 1],
                device_id={"ctx": rowdev(d)},
                device_id_type=MESH,
            )
            for i, (src, dst) in enumerate(((ssend, srecv), (tsend, trecv)))
        ]

    def r_copies(d):
        return [
            pltpu.make_async_remote_copy(
                src_ref=src,
                dst_ref=dst.at[d - 1],
                send_sem=r_send.at[i, d - 1],
                recv_sem=r_recv.at[i, d - 1],
                device_id={"ctx": ((z + d) % zn) * ROW + x},
                device_id_type=MESH,
            )
            for i, (src, dst) in enumerate(((rsend, rrecv), (trsend, trrecv)))
        ]

    def a_copy(d):
        return pltpu.make_async_remote_copy(
            src_ref=asend,
            dst_ref=arecv,
            send_sem=a_send.at[d - 1],
            recv_sem=a_recv.at[0],
            device_id={"ctx": ((z + d) % zn) * ROW + x},
            device_id_type=MESH,
        )

    def l_used(m, block):
        if m < 3:
            return z // 2**m % 2 == 1
        return block >= 1 if m == 3 else block == 3

    def l_copy(m, d, source):
        return pltpu.make_async_remote_copy(
            src_ref=lsend.at[d, m],
            dst_ref=lrecv.at[source, m],
            send_sem=l_send.at[m, d - 1],
            recv_sem=l_recv.at[m, d - 1],
            device_id={"ctx": rowdev(d)},
            device_id_type=MESH,
        )

    def n_copy(d):
        return pltpu.make_async_remote_copy(
            src_ref=nsend,
            dst_ref=nrecv.at[d - 1],
            send_sem=n_send.at[d - 1],
            recv_sem=n_recv.at[d - 1],
            device_id={"head": (mh + d) % hn},
            device_id_type=MESH,
        )

    def o_copy(j):
        return pltpu.make_async_remote_copy(
            src_ref=obuf.at[j],
            dst_ref=ao_hbm.at[:, cols(x)],
            send_sem=o_send.at[j],
            recv_sem=o_recv.at[x],
            device_id={"ctx": z * ROW + j},
            device_id_type=MESH,
        )

    def o_local(j):
        return pltpu.make_async_copy(obuf.at[j], ao_hbm.at[:, cols(x)], out_sem.at[1])

    pl.semaphore_wait(barrier, ROW - 1 + zl + z // 4 + hn - 1)
    for d in reaches:

        @pl.when(hears_from(d))
        def _():
            pl.semaphore_signal(
                ready.at[d - 1], inc=1, device_id={"ctx": (z - d) * ROW + x}, device_id_type=MESH
            )

    for d in (1, 3):
        x_copy(0, d).start()

    decay_in.wait()
    lane = lax.broadcasted_iota(jnp.int32, (8, tok), 1)
    cum = jnp.concatenate([ldbuf[...], jnp.zeros((8 - ROW, tok), F32)], axis=0)
    shift = 1
    while shift < tok:
        cum = cum + jnp.where(lane >= shift, pltpu.roll(cum, shift, axis=1), 0.0)
        shift *= 2
    last = cum[:, tok - 1 : tok]
    tail = jnp.exp(last - cum)
    reach = jnp.exp(cum)
    gates_in.wait()
    for h in range(ROW):
        grow[h, 0:20, :] = lgbuf[:, h, :]
        grow[h, 20:21, :] = cum[h : h + 1]
        grow[h, 21:22, :] = tail[h : h + 1]
        grow[h, 22:23, :] = reach[h : h + 1]
        grow[h, 23:24, :] = cum[h : h + 1]
        grow[h, 24:32, :] = cum
        tsend[h] = jnp.broadcast_to(last[h : h + 1], (8, 128))
        gcol[h] = grow[h].T

    state_in[0].wait()
    state_in[1].wait()

    def summary(h, _):
        kf = sk[:, cols(h)].astype(F32)
        low = (kf * gcol[h, :, 21:22]).astype(BF16)
        ssend[h] = tn_dot(low, sv[:, cols(h)]).astype(BF16)
        return 0

    lax.fori_loop(0, ROW, summary, 0)
    for d in (1, 3, 2):
        for c in s_copies(d):
            c.start()
    for t, d in ((1, 1), (1, 3), (0, 2), (1, 2), (2, 1), (2, 3), (2, 2)):
        x_copy(t, d).start()
    own_halo = (x >= 1) & (z < zn - 1)

    @pl.when(z < zn - 1)
    def _():
        pl.semaphore_wait(ready.at[0], 1)

    @pl.when(own_halo)
    def _():
        halo_own(0).start()

    srecv[x] = ssend[x]
    trecv[x] = tsend[x]

    state_in[2].wait()
    state_in[3].wait()
    row_i = lax.broadcasted_iota(jnp.int32, (chunk, chunk), 0)
    col_i = lax.broadcasted_iota(jnp.int32, (chunk, chunk), 1)

    def relay(t, d):
        x_wait(t, d)

        @pl.when(relay_if(d))
        def _():
            halo_relay(t, d).start()

    apart = row_i ^ col_i

    def inside(h, _):
        hc = cols(h)
        crow = grow[h, 20:21, :]
        for i in range(chunks):
            rows = pl.ds(i * chunk, chunk)
            g = gcol[h, rows, :]
            ccol = g[:, 20:21]
            scores = nt_dot(sq[rows, hc], sk[0 : (i + 1) * chunk, hc])
            parts = []
            for j in range(i + 1):
                s = scores[:, j * chunk : (j + 1) * chunk]
                gap = ccol - crow[:, j * chunk : (j + 1) * chunk]
                if j < i:
                    level = (i ^ j).bit_length() + 7
                    m = s * jnp.exp(gap) * g[:, level : level + 1]
                else:
                    gate = jnp.broadcast_to(g[:, 0:1], (chunk, chunk))
                    for level in range(1, 8):
                        gate = jnp.where(apart >= 1 << (level - 1), g[:, level : level + 1], gate)
                    seen = row_i >= col_i
                    m = jnp.where(seen, s * jnp.exp(jnp.where(seen, gap, 0.0)) * gate, 0.0)
                parts.append(m.astype(BF16))
            low = parts[0] if i == 0 else jnp.concatenate(parts, axis=1)
            mixed[h, rows, :] = jnp.dot(
                low, sv[0 : (i + 1) * chunk, hc], preferred_element_type=F32
            )
        return 0

    lax.fori_loop(0, ROW // 2, inside, 0)
    relay(0, 1)
    relay(0, 3)
    lax.fori_loop(ROW // 2, ROW, inside, 0)

    def reaching(h, _):
        hc = cols(h)
        for i in range(chunks):
            rows = pl.ds(i * chunk, chunk)
            g = gcol[h, rows, :]
            qf = sq[rows, hc].astype(F32) * g[:, 22:23]
            near = jnp.where(x == 2, g[:, 11:12], g[:, 10:11])
            for m, gate in enumerate((g[:, 12:13], g[:, 13:14], g[:, 14:15], near, g[:, 11:12])):
                reached[h, rows, m * hd : (m + 1) * hd] = (qf * gate).astype(BF16)
            v = sg[rows, hc].astype(F32)
            gated[rows, hc] = v / (1.0 + jnp.exp(-v))
        return 0

    for d in range(1, ROW):
        p = (x + ROW - d) % ROW
        for i, (src, dst) in enumerate(((ssend, srecv), (tsend, trecv))):
            pltpu.make_async_remote_copy(
                src_ref=src.at[p],
                dst_ref=dst.at[p],
                send_sem=s_send.at[i, d - 1],
                recv_sem=s_recv.at[i, d - 1],
                device_id={"ctx": rowdev(d)},
                device_id_type=MESH,
            ).wait_recv()
    tot = [trecv[i] for i in range(ROW)]
    st = [srecv[i].astype(F32) for i in range(ROW)]
    pair = st[0] * jnp.exp(tot[1][0:1]) + st[1]
    row_state = (
        pair * jnp.exp((tot[2] + tot[3])[0:1]) + st[2] * jnp.exp(tot[3][0:1]) + st[3]
    )
    rsend[...] = row_state.astype(BF16)
    trsend[...] = tot[0] + tot[1] + tot[2] + tot[3]
    for d in reaches:
        if d > 1:

            @pl.when(sends_to(d))
            def _():
                pl.semaphore_wait(ready.at[d - 1], 1)

    for d in group:

        @pl.when(zl + d < 4)
        def _():
            for c in r_copies(d):
                c.start()


    @pl.when(own_halo)
    def _():
        halo_own(1).start()

    lax.fori_loop(0, ROW, reaching, 0)

    for d in group:

        @pl.when(zl >= d)
        def _():
            for c in r_copies(d):
                c.wait_recv()

    levels = [jnp.zeros((hd, hd), F32) for _ in range(2)]
    decay = jnp.zeros((8, 128), F32)
    for d in group:
        near2 = (zl + 4) // 2 == (zl + 4 - d) // 2
        w = jnp.exp(decay)[0:1]
        held = rrecv[d - 1].astype(F32)
        levels[0] = levels[0] + jnp.where(near2, w, 0.0) * held
        levels[1] = levels[1] + jnp.where(near2, 0.0, w) * held
        decay = decay + trrecv[d - 1]
    asend[...] = (
        (levels[0] + levels[1]) * jnp.exp(trsend[0:1]) + row_state
    ).astype(BF16)
    for d in reaches:

        @pl.when((z == 3) & sends_to(d))
        def _():
            a_copy(d).start()

    def before(xp):
        return (
            jnp.where(xp >= 1, tot[0], 0.0)
            + jnp.where(xp >= 2, tot[1], 0.0)
            + jnp.where(xp >= 3, tot[2], 0.0)
        )

    def l_start(d, slots):
        for m in slots:

            @pl.when(l_used(m, (x + d) % ROW))
            def _():
                l_copy(m, d, x).start()

    for d in (0, 1, 3, 2):
        xp = (x + d) % ROW
        w = jnp.exp(before(xp))[0:1]
        for m in range(2):
            lsend[d, m] = (levels[m] * w).astype(BF16)
        near = jnp.where(xp == 1, st[0], jnp.where(xp == 2, pair, jnp.where(xp == 3, st[2], 0.0)))
        lsend[d, 3] = near.astype(BF16)
        lsend[d, 4] = (pair * jnp.exp(tot[2][0:1])).astype(BF16)
        if d > 0:
            l_start(d, (0, 1, 3, 4))

    for t, d in ((1, 1), (1, 3), (0, 2), (1, 2)):
        relay(t, d)

    @pl.when(z >= 4)
    def _():
        pltpu.make_async_remote_copy(
            src_ref=asend,
            dst_ref=arecv,
            send_sem=a_send.at[0],
            recv_sem=a_recv.at[0],
            device_id={"ctx": ((z + 1) % zn) * ROW + x},
            device_id_type=MESH,
        ).wait_recv()

    whole = arecv[...].astype(F32)
    for d in (0, 1, 3, 2):
        w = jnp.exp(before((x + d) % ROW) + decay)[0:1]
        lsend[d, 2] = (whole * w).astype(BF16)
        if d > 0:
            l_start(d, (2,))

    lrecv[x, 0:4] = lsend[0, 0:4]

    @pl.when(x == 3)
    def _():
        lrecv[x, 4] = lsend[0, 4]

    for c in own_in:
        c.wait()

    kappa = math.log2(math.e) / math.sqrt(hd)
    qrows = 256
    absent = jnp.where(z == 0, NEG, 0.0).astype(F32)

    def attend(j):
        def body(i, _):
            first = pl.multiple_of(i * qrows, qrows)
            q = qbuf[j, pl.ds(first, qrows), :]
            logits = []
            for s in range(ROW):
                part = nt_dot(q, kbuf[j + s])
                if s < 3:
                    part = part + jnp.where(j + s < 3, absent, 0.0)
                if s == ROW - 1:
                    r = lax.broadcasted_iota(jnp.int32, (qrows, tok), 0) + first
                    c = lax.broadcasted_iota(jnp.int32, (qrows, tok), 1)
                    part = jnp.where(r >= c, part, NEG)
                logits.append(part)
            top = jnp.maximum(
                jnp.maximum(logits[0], logits[1]), jnp.maximum(logits[2], logits[3])
            )
            top = jnp.max(top, axis=1, keepdims=True)
            weights = [jnp.exp2((part - top) * kappa) for part in logits]
            total = jnp.sum(
                (weights[0] + weights[1]) + (weights[2] + weights[3]), axis=1, keepdims=True
            )
            out = None
            for s in range(ROW):
                term = jnp.dot(
                    weights[s].astype(BF16), vbuf[j + s], preferred_element_type=F32
                )
                out = term if out is None else out + term
            obuf[j, pl.ds(first, qrows), :] = (out / total).astype(BF16)
            return 0

        lax.fori_loop(0, tok // qrows, body, 0)

    turns = (
        jnp.where(x < 2, 3, x - 1),
        jnp.where(x == 0, 2, jnp.where(x == 3, 1, 0)),
        (x + 1) % ROW,
        x,
    )

    def step(k):
        j = turns[k]
        done = ROW - 1
        for earlier in turns[:k]:
            done = jnp.minimum(done, earlier)
        for slot in (2, 1, 0):

            @pl.when((z > 0) & (slot >= j) & (slot < done))
            def _():
                for t in (0, 1):
                    halo_wait(t, slot)

        if k < ROW - 1:
            d = (x + ROW - j) % ROW
            x_wait(2, d)
        attend(j)
        if k < ROW - 1:
            o_copy(j).start()
        else:
            o_local(j).start()

    step(0)

    step(1)

    step(2)

    for d in range(1, ROW):
        for m in range(5):

            @pl.when(l_used(m, x))
            def _():
                l_copy(m, d, (x + ROW - d) % ROW).wait_recv()

    def across(h, acc):
        hc = cols(h)
        squares = []
        states = lrecv[h].reshape(5 * hd, hd)
        for i in range(chunks):
            rows = pl.ds(i * chunk, chunk)
            far = jnp.dot(reached[h, rows, :], states, preferred_element_type=F32)
            out = (mixed[h, rows, :] + far) * gated[rows, hc]
            gated[rows, hc] = out
            squares.append(out * out)
        return tuple(a + s for a, s in zip(acc, squares))

    acc = lax.fori_loop(
        0, ROW, across, tuple(jnp.zeros((chunk, hd), F32) for _ in range(chunks))
    )
    nsend[...] = jnp.zeros_like(nsend)
    for i in range(chunks):
        nsend[i : i + 1, :] = jnp.sum(acc[i].T, axis=0, keepdims=True)
    for d in range(1, hn):
        n_copy(d).start()

    step(3)

    total = nsend[...]
    for d in range(1, hn):
        n_copy(d).wait_recv()
        total = total + nrecv[d - 1]
    gain_in.wait()
    scale = lax.rsqrt(total / (hn * ROW * hd) + 1e-05)
    for i in range(chunks):
        rows = pl.ds(i * chunk, chunk)
        scale_col = jnp.broadcast_to(scale[i : i + 1], (chunk, chunk)).T
        for h in range(ROW):
            hs = slice(h * hd, (h + 1) * hd)
            mout[rows, hs] = (gated[rows, hs] * scale_col * gainbuf[:, hs]).astype(BF16)
    mix_out = pltpu.make_async_copy(mout, mo_hbm, out_sem.at[0])
    mix_out.start()

    for d in range(1, ROW):
        for t in range(3):
            x_copy(t, d).wait_send()
        for c in s_copies(d):
            c.wait_send()
        for m in range(5):

            @pl.when(l_used(m, (x + d) % ROW))
            def _():
                l_copy(m, d, x).wait_send()

        @pl.when(relay_if(d))
        def _():
            for t in (0, 1):
                halo_relay(t, d).wait_send()

    @pl.when(own_halo)
    def _():
        for t in (0, 1):
            halo_own(t).wait_send()

    for d in group:

        @pl.when(zl + d < 4)
        def _():
            for c in r_copies(d):
                c.wait_send()

    for d in reaches:

        @pl.when((z == 3) & sends_to(d))
        def _():
            a_copy(d).wait_send()

    for d in range(1, hn):
        n_copy(d).wait_send()
    for j in range(ROW):

        @pl.when(x != j)
        def _():
            o_copy(j).wait_send()
            pltpu.make_async_remote_copy(
                src_ref=obuf.at[j],
                dst_ref=ao_hbm.at[:, cols(j)],
                send_sem=o_send.at[j],
                recv_sem=o_recv.at[j],
                device_id={"ctx": z * ROW + j},
                device_id_type=MESH,
            ).wait_recv()

        @pl.when(x == j)
        def _():
            o_local(j).wait()

    mix_out.wait()


def hbm(*arrays):
    return [pltpu.with_memory_space_constraint(a, pltpu.HBM) for a in arrays]


def shards(zn, hn, sq, sk, sv, sg, ld, lg, gain, aq, ak, av):
    tok = sq.shape[0]
    heads = ld.shape[0]
    hd = sq.shape[1] // heads
    wide = heads * hd
    dma = pltpu.SemaphoreType.DMA
    vm = pltpu.VMEM
    anywhere = pl.BlockSpec(memory_space=pltpu.HBM)
    out = jax.ShapeDtypeStruct((tok, wide), BF16)
    return pl.pallas_call(
        functools.partial(kernel, zn, hn),
        out_shape=(out, out),
        in_specs=[anywhere] * 10,
        out_specs=(anywhere, anywhere),
        scratch_shapes=[
            vm((tok, wide), BF16),
            vm((tok, wide), BF16),
            vm((tok, wide), BF16),
            vm((tok, wide), BF16),
            vm((4, tok, hd), BF16),
            vm((7, tok, hd), BF16),
            vm((7, tok, hd), BF16),
            vm((4, tok, hd), BF16),
            vm((lg.shape[1], heads, tok), F32),
            vm((heads, tok), F32),
            vm((1, wide), F32),
            vm((heads, 32, tok), F32),
            vm((heads, tok, 32), F32),
            vm((heads, tok, hd), F32),
            vm((tok, wide), F32),
            vm((heads, tok, 5 * hd), BF16),
            vm((tok, wide), BF16),
            vm((4, hd, hd), BF16),
            vm((4, hd, hd), BF16),
            vm((4, 8, 128), F32),
            vm((4, 8, 128), F32),
            vm((hd, hd), BF16),
            vm((3, hd, hd), BF16),
            vm((8, 128), F32),
            vm((3, 8, 128), F32),
            vm((hd, hd), BF16),
            vm((hd, hd), BF16),
            vm((4, 5, hd, hd), BF16),
            vm((4, 5, hd, hd), BF16),
            vm((8, 128), F32),
            vm((max(hn - 1, 1), 8, 128), F32),
            dma((10,)),
            dma((3, 3)),
            dma((3, 3)),
            dma((2, 4)),
            dma((2, 4)),
            dma((2, 3)),
            dma((2, 3)),
            dma((2, 3)),
            dma((2, 3)),
            dma((5, 3)),
            dma((5, 3)),
            dma((max(hn - 1, 1),)),
            dma((max(hn - 1, 1),)),
            dma((4,)),
            dma((4,)),
            dma((2,)),
            pltpu.SemaphoreType.REGULAR((4,)),
            dma((4,)),
            dma((1,)),
        ],
        compiler_params=pltpu.CompilerParams(
            collective_id=0, has_side_effects=True, vmem_limit_bytes=48 * 1024 * 1024
        ),
        cost_estimate=pl.CostEstimate(
            flops=3_000_000_000, bytes_accessed=5_000_000, transcendentals=5_000_000
        ),
    )(*hbm(sq, sk, sv, sg, ld, jnp.transpose(lg, (1, 0, 2)), gain.reshape(1, wide), aq, ak, av))


def solution(mesh):
    zn = mesh.shape["ctx"] // ROW
    hn = mesh.shape["head"]
    return jax.shard_map(
        functools.partial(shards, zn, hn),
        mesh=mesh,
        in_specs=(
            P("ctx", "head"),
            P("ctx", "head"),
            P("ctx", "head"),
            P("ctx", "head"),
            P("head", "ctx"),
            P("head", None, "ctx"),
            P("head"),
            P("ctx", "head"),
            P("ctx", "head"),
            P("ctx", "head"),
        ),
        out_specs=(P("ctx", "head"), P("ctx", "head")),
        check_vma=False,
    )
```

```python
import functools
import math

import jax
import jax.numpy as jnp
from jax import lax
from jax.experimental import pallas as pl
from jax.experimental.pallas import tpu as pltpu
from jax.sharding import PartitionSpec as P

MESH = pl.DeviceIdType.MESH
ROW = 4
F32 = jnp.float32
BF16 = jnp.bfloat16
NEG = -1e30


def nt_dot(a, b):
    return lax.dot_general(a, b, (((1,), (1,)), ((), ())), preferred_element_type=F32)


def tn_dot(a, b):
    return lax.dot_general(a, b, (((0,), (0,)), ((), ())), preferred_element_type=F32)


def kernel(
    zn,
    hn,
    sq_hbm,
    sk_hbm,
    sv_hbm,
    sg_hbm,
    ld_hbm,
    lg_hbm,
    gain_hbm,
    aq_hbm,
    ak_hbm,
    av_hbm,
    mo_hbm,
    ao_hbm,
    sq,
    sk,
    sv,
    sg,
    qbuf,
    kbuf,
    vbuf,
    obuf,
    lgbuf,
    ldbuf,
    gainbuf,
    grow,
    gcol,
    mixed,
    gated,
    reached,
    mout,
    ssend,
    srecv,
    tsend,
    trecv,
    rsend,
    rrecv,
    trsend,
    trrecv,
    asend,
    arecv,
    lsend,
    lrecv,
    nsend,
    nrecv,
    loc_sem,
    x_send,
    x_recv,
    h_send,
    h_recv,
    s_send,
    s_recv,
    r_send,
    r_recv,
    l_send,
    l_recv,
    n_send,
    n_recv,
    o_send,
    o_recv,
    out_sem,
    mix_sem,
    ready,
    a_send,
    a_recv,
):
    me = lax.axis_index("ctx")
    mh = lax.axis_index("head")
    z = me // ROW
    x = me % ROW
    tok = qbuf.shape[1]
    hd = qbuf.shape[2]
    chunk = 128
    chunks = tok // chunk

    def rowdev(d):
        return z * ROW + (x + d) % ROW

    def cols(h):
        return pl.ds(pl.multiple_of(h * hd, hd), hd)

    zl = z % 4

    def sends_to(d):
        return ((zl + d < 4) | (z == 3)) & (z + d < zn)

    def hears_from(d):
        return (zl >= d) | (z - d == 3)

    reaches = range(1, min(zn, 5))
    group = range(1, min(zn, 4))

    rrecv[...] = jnp.zeros_like(rrecv)
    arecv[...] = jnp.zeros_like(arecv)
    trrecv[...] = jnp.zeros_like(trrecv)

    lrecv[...] = jnp.zeros_like(lrecv)

    @pl.when(z == 0)
    def _():
        kbuf[0:3] = jnp.zeros((3, tok, hd), BF16)
        vbuf[0:3] = jnp.zeros((3, tok, hd), BF16)

    barrier = pltpu.get_barrier_semaphore()
    for d in range(1, ROW):
        pl.semaphore_signal(barrier, inc=1, device_id={"ctx": rowdev(d)}, device_id_type=MESH)
    for d in reaches:

        @pl.when(sends_to(d))
        def _():
            pl.semaphore_signal(
                barrier, inc=1, device_id={"ctx": (z + d) * ROW + x}, device_id_type=MESH
            )

    for d in range(1, hn):
        pl.semaphore_signal(barrier, inc=1, device_id={"head": (mh + d) % hn}, device_id_type=MESH)

    state_in = [
        pltpu.make_async_copy(src, dst, loc_sem.at[i])
        for i, (src, dst) in enumerate(((sk_hbm, sk), (sv_hbm, sv), (sq_hbm, sq), (sg_hbm, sg)))
    ]
    gates_in = pltpu.make_async_copy(lg_hbm, lgbuf, loc_sem.at[7])
    decay_in = pltpu.make_async_copy(ld_hbm, ldbuf, loc_sem.at[8])
    gain_in = pltpu.make_async_copy(gain_hbm, gainbuf, loc_sem.at[9])
    decay_in.start()
    gates_in.start()
    for c in state_in:
        c.start()
    gain_in.start()
    att = ((ak_hbm, kbuf, 3), (av_hbm, vbuf, 3), (aq_hbm, qbuf, 0))
    own_in = [
        pltpu.make_async_copy(src.at[:, cols(x)], dst.at[base + x], loc_sem.at[4 + i])
        for i, (src, dst, base) in enumerate(att)
    ]
    for c in own_in:
        c.start()

    def x_copy(t, d):
        src, dst, base = att[t]
        return pltpu.make_async_remote_copy(
            src_ref=src.at[:, cols((x + d) % ROW)],
            dst_ref=dst.at[base + x],
            send_sem=x_send.at[t, d - 1],
            recv_sem=x_recv.at[t, d - 1],
            device_id={"ctx": rowdev(d)},
            device_id_type=MESH,
        )

    def x_wait(t, d):
        src, dst, base = att[t]
        pltpu.make_async_remote_copy(
            src_ref=src.at[:, cols((x + d) % ROW)],
            dst_ref=dst.at[base + (x + ROW - d) % ROW],
            send_sem=x_send.at[t, d - 1],
            recv_sem=x_recv.at[t, d - 1],
            device_id={"ctx": rowdev(d)},
            device_id_type=MESH,
        ).wait_recv()

    def halo_own(t):
        src, dst, _ = att[t]
        return pltpu.make_async_remote_copy(
            src_ref=src.at[:, cols(x)],
            dst_ref=dst.at[(x + ROW - 1) % ROW],
            send_sem=h_send.at[t, 0],
            recv_sem=h_recv.at[t, (x + ROW - 1) % ROW],
            device_id={"ctx": me + ROW},
            device_id_type=MESH,
        )

    def halo_relay(t, d):
        dst = att[t][1]
        block = (x + ROW - d) % ROW
        return pltpu.make_async_remote_copy(
            src_ref=dst.at[3 + block],
            dst_ref=dst.at[(block + ROW - 1) % ROW],
            send_sem=h_send.at[t, d],
            recv_sem=h_recv.at[t, (block + ROW - 1) % ROW],
            device_id={"ctx": me + ROW},
            device_id_type=MESH,
        )

    def relay_if(d):
        return ((x + ROW - d) % ROW >= 1) & (z < zn - 1)

    def halo_wait(t, slot):
        dst = att[t][1]
        pltpu.make_async_remote_copy(
            src_ref=dst.at[slot],
            dst_ref=dst.at[slot],
            send_sem=h_send.at[t, 0],
            recv_sem=h_recv.at[t, slot],
            device_id={"ctx": (me + ROW) % (zn * ROW)},
            device_id_type=MESH,
        ).wait_recv()

    def s_copies(d):
        p = (x + d) % ROW
        return [
            pltpu.make_async_remote_copy(
                src_ref=src.at[p],
                dst_ref=dst.at[x],
                send_sem=s_send.at[i, d - 1],
                recv_sem=s_recv.at[i, d - 1],
                device_id={"ctx": rowdev(d)},
                device_id_type=MESH,
            )
            for i, (src, dst) in enumerate(((ssend, srecv), (tsend, trecv)))
        ]

    def r_copies(d):
        return [
            pltpu.make_async_remote_copy(
                src_ref=src,
                dst_ref=dst.at[d - 1],
                send_sem=r_send.at[i, d - 1],
                recv_sem=r_recv.at[i, d - 1],
                device_id={"ctx": ((z + d) % zn) * ROW + x},
                device_id_type=MESH,
            )
            for i, (src, dst) in enumerate(((rsend, rrecv), (trsend, trrecv)))
        ]

    def a_copy(d):
        return pltpu.make_async_remote_copy(
            src_ref=asend,
            dst_ref=arecv,
            send_sem=a_send.at[d - 1],
            recv_sem=a_recv.at[0],
            device_id={"ctx": ((z + d) % zn) * ROW + x},
            device_id_type=MESH,
        )

    def l_used(m, block):
        if m < 3:
            return z // 2**m % 2 == 1
        return block >= 1 if m == 3 else block == 3

    def l_copy(m, d, source):
        return pltpu.make_async_remote_copy(
            src_ref=lsend.at[d, m],
            dst_ref=lrecv.at[source, m],
            send_sem=l_send.at[m, d - 1],
            recv_sem=l_recv.at[m, d - 1],
            device_id={"ctx": rowdev(d)},
            device_id_type=MESH,
        )

    def n_copy(d):
        return pltpu.make_async_remote_copy(
            src_ref=nsend,
            dst_ref=nrecv.at[d - 1],
            send_sem=n_send.at[d - 1],
            recv_sem=n_recv.at[d - 1],
            device_id={"head": (mh + d) % hn},
            device_id_type=MESH,
        )

    def o_copy(j):
        return pltpu.make_async_remote_copy(
            src_ref=obuf.at[j],
            dst_ref=ao_hbm.at[:, cols(x)],
            send_sem=o_send.at[j],
            recv_sem=o_recv.at[x],
            device_id={"ctx": z * ROW + j},
            device_id_type=MESH,
        )

    def o_local(j):
        return pltpu.make_async_copy(obuf.at[j], ao_hbm.at[:, cols(x)], out_sem.at[1])

    pl.semaphore_wait(barrier, ROW - 1 + zl + z // 4 + hn - 1)
    for d in reaches:

        @pl.when(hears_from(d))
        def _():
            pl.semaphore_signal(
                ready.at[d - 1], inc=1, device_id={"ctx": (z - d) * ROW + x}, device_id_type=MESH
            )

    for d in (1, 3):
        x_copy(0, d).start()

    decay_in.wait()
    lane = lax.broadcasted_iota(jnp.int32, (8, tok), 1)
    cum = jnp.concatenate([ldbuf[...], jnp.zeros((8 - ROW, tok), F32)], axis=0)
    shift = 1
    while shift < tok:
        cum = cum + jnp.where(lane >= shift, pltpu.roll(cum, shift, axis=1), 0.0)
        shift *= 2
    last = cum[:, tok - 1 : tok]
    tail = jnp.exp(last - cum)
    reach = jnp.exp(cum)
    gates_in.wait()
    for h in range(ROW):
        grow[h, 0:20, :] = lgbuf[:, h, :]
        grow[h, 20:21, :] = cum[h : h + 1]
        grow[h, 21:22, :] = tail[h : h + 1]
        grow[h, 22:23, :] = reach[h : h + 1]
        grow[h, 23:24, :] = cum[h : h + 1]
        grow[h, 24:32, :] = cum
        tsend[h] = jnp.broadcast_to(last[h : h + 1], (8, 128))
        gcol[h] = grow[h].T

    state_in[0].wait()
    state_in[1].wait()

    def summary(h, _):
        kf = sk[:, cols(h)].astype(F32)
        low = (kf * gcol[h, :, 21:22]).astype(BF16)
        ssend[h] = tn_dot(low, sv[:, cols(h)]).astype(BF16)
        return 0

    lax.fori_loop(0, ROW, summary, 0)
    for d in (1, 3, 2):
        for c in s_copies(d):
            c.start()
    for t, d in ((1, 1), (1, 3), (0, 2), (1, 2), (2, 1), (2, 3), (2, 2)):
        x_copy(t, d).start()
    own_halo = (x >= 1) & (z < zn - 1)

    @pl.when(z < zn - 1)
    def _():
        pl.semaphore_wait(ready.at[0], 1)

    @pl.when(own_halo)
    def _():
        halo_own(0).start()

    srecv[x] = ssend[x]
    trecv[x] = tsend[x]

    state_in[2].wait()
    state_in[3].wait()
    row_i = lax.broadcasted_iota(jnp.int32, (chunk, chunk), 0)
    col_i = lax.broadcasted_iota(jnp.int32, (chunk, chunk), 1)

    def relay(t, d):
        x_wait(t, d)

        @pl.when(relay_if(d))
        def _():
            halo_relay(t, d).start()

    apart = row_i ^ col_i

    def inside(h, _):
        hc = cols(h)
        crow = grow[h, 20:21, :]
        for i in range(chunks):
            rows = pl.ds(i * chunk, chunk)
            g = gcol[h, rows, :]
            ccol = g[:, 20:21]
            scores = nt_dot(sq[rows, hc], sk[0 : (i + 1) * chunk, hc])
            parts = []
            for j in range(i + 1):
                s = scores[:, j * chunk : (j + 1) * chunk]
                gap = ccol - crow[:, j * chunk : (j + 1) * chunk]
                if j < i:
                    level = (i ^ j).bit_length() + 7
                    m = s * jnp.exp(gap) * g[:, level : level + 1]
                else:
                    gate = jnp.broadcast_to(g[:, 0:1], (chunk, chunk))
                    for level in range(1, 8):
                        gate = jnp.where(apart >= 1 << (level - 1), g[:, level : level + 1], gate)
                    seen = row_i >= col_i
                    m = jnp.where(seen, s * jnp.exp(jnp.where(seen, gap, 0.0)) * gate, 0.0)
                parts.append(m.astype(BF16))
            low = parts[0] if i == 0 else jnp.concatenate(parts, axis=1)
            mixed[h, rows, :] = jnp.dot(
                low, sv[0 : (i + 1) * chunk, hc], preferred_element_type=F32
            )
        return 0

    lax.fori_loop(0, ROW // 2, inside, 0)
    relay(0, 1)
    relay(0, 3)
    lax.fori_loop(ROW // 2, ROW, inside, 0)

    def reaching(h, _):
        hc = cols(h)
        for i in range(chunks):
            rows = pl.ds(i * chunk, chunk)
            g = gcol[h, rows, :]
            qf = sq[rows, hc].astype(F32) * g[:, 22:23]
            near = jnp.where(x == 2, g[:, 11:12], g[:, 10:11])
            for m, gate in enumerate((g[:, 12:13], g[:, 13:14], g[:, 14:15], near, g[:, 11:12])):
                reached[h, rows, m * hd : (m + 1) * hd] = (qf * gate).astype(BF16)
            v = sg[rows, hc].astype(F32)
            gated[rows, hc] = v / (1.0 + jnp.exp(-v))
        return 0

    for d in range(1, ROW):
        p = (x + ROW - d) % ROW
        for i, (src, dst) in enumerate(((ssend, srecv), (tsend, trecv))):
            pltpu.make_async_remote_copy(
                src_ref=src.at[p],
                dst_ref=dst.at[p],
                send_sem=s_send.at[i, d - 1],
                recv_sem=s_recv.at[i, d - 1],
                device_id={"ctx": rowdev(d)},
                device_id_type=MESH,
            ).wait_recv()
    tot = [trecv[i] for i in range(ROW)]
    st = [srecv[i].astype(F32) for i in range(ROW)]
    pair = st[0] * jnp.exp(tot[1][0:1]) + st[1]
    row_state = (
        pair * jnp.exp((tot[2] + tot[3])[0:1]) + st[2] * jnp.exp(tot[3][0:1]) + st[3]
    )
    rsend[...] = row_state.astype(BF16)
    trsend[...] = tot[0] + tot[1] + tot[2] + tot[3]
    for d in reaches:
        if d > 1:

            @pl.when(sends_to(d))
            def _():
                pl.semaphore_wait(ready.at[d - 1], 1)

    for d in group:

        @pl.when(zl + d < 4)
        def _():
            for c in r_copies(d):
                c.start()


    @pl.when(own_halo)
    def _():
        halo_own(1).start()

    lax.fori_loop(0, ROW, reaching, 0)

    for d in group:

        @pl.when(zl >= d)
        def _():
            for c in r_copies(d):
                c.wait_recv()

    levels = [jnp.zeros((hd, hd), F32) for _ in range(2)]
    decay = jnp.zeros((8, 128), F32)
    for d in group:
        near2 = (zl + 4) // 2 == (zl + 4 - d) // 2
        w = jnp.exp(decay)[0:1]
        held = rrecv[d - 1].astype(F32)
        levels[0] = levels[0] + jnp.where(near2, w, 0.0) * held
        levels[1] = levels[1] + jnp.where(near2, 0.0, w) * held
        decay = decay + trrecv[d - 1]
    asend[...] = (
        (levels[0] + levels[1]) * jnp.exp(trsend[0:1]) + row_state
    ).astype(BF16)
    for d in reaches:

        @pl.when((z == 3) & sends_to(d))
        def _():
            a_copy(d).start()

    def before(xp):
        return (
            jnp.where(xp >= 1, tot[0], 0.0)
            + jnp.where(xp >= 2, tot[1], 0.0)
            + jnp.where(xp >= 3, tot[2], 0.0)
        )

    def l_start(d, slots):
        for m in slots:

            @pl.when(l_used(m, (x + d) % ROW))
            def _():
                l_copy(m, d, x).start()

    for d in (0, 1, 3, 2):
        xp = (x + d) % ROW
        w = jnp.exp(before(xp))[0:1]
        for m in range(2):
            lsend[d, m] = (levels[m] * w).astype(BF16)
        near = jnp.where(xp == 1, st[0], jnp.where(xp == 2, pair, jnp.where(xp == 3, st[2], 0.0)))
        lsend[d, 3] = near.astype(BF16)
        lsend[d, 4] = (pair * jnp.exp(tot[2][0:1])).astype(BF16)
        if d > 0:
            l_start(d, (0, 1, 3, 4))

    for t, d in ((1, 1), (1, 3), (0, 2), (1, 2)):
        relay(t, d)

    @pl.when(z >= 4)
    def _():
        pltpu.make_async_remote_copy(
            src_ref=asend,
            dst_ref=arecv,
            send_sem=a_send.at[0],
            recv_sem=a_recv.at[0],
            device_id={"ctx": ((z + 1) % zn) * ROW + x},
            device_id_type=MESH,
        ).wait_recv()

    whole = arecv[...].astype(F32)
    for d in (0, 1, 3, 2):
        w = jnp.exp(before((x + d) % ROW) + decay)[0:1]
        lsend[d, 2] = (whole * w).astype(BF16)
        if d > 0:
            l_start(d, (2,))

    lrecv[x, 0:4] = lsend[0, 0:4]

    @pl.when(x == 3)
    def _():
        lrecv[x, 4] = lsend[0, 4]

    for c in own_in:
        c.wait()

    kappa = math.log2(math.e) / math.sqrt(hd)
    qrows = 256
    absent = jnp.where(z == 0, NEG, 0.0).astype(F32)

    def attend(j):
        def body(i, _):
            first = pl.multiple_of(i * qrows, qrows)
            q = qbuf[j, pl.ds(first, qrows), :]
            logits = []
            for s in range(ROW):
                part = nt_dot(q, kbuf[j + s])
                if s < 3:
                    part = part + jnp.where(j + s < 3, absent, 0.0)
                if s == ROW - 1:
                    r = lax.broadcasted_iota(jnp.int32, (qrows, tok), 0) + first
                    c = lax.broadcasted_iota(jnp.int32, (qrows, tok), 1)
                    part = jnp.where(r >= c, part, NEG)
                logits.append(part)
            top = jnp.maximum(
                jnp.maximum(logits[0], logits[1]), jnp.maximum(logits[2], logits[3])
            )
            top = jnp.max(top, axis=1, keepdims=True)
            weights = [jnp.exp2((part - top) * kappa) for part in logits]
            total = jnp.sum(
                (weights[0] + weights[1]) + (weights[2] + weights[3]), axis=1, keepdims=True
            )
            out = None
            for s in range(ROW):
                term = jnp.dot(
                    weights[s].astype(BF16), vbuf[j + s], preferred_element_type=F32
                )
                out = term if out is None else out + term
            obuf[j, pl.ds(first, qrows), :] = (out / total).astype(BF16)
            return 0

        lax.fori_loop(0, tok // qrows, body, 0)

    turns = (
        jnp.where(x < 2, 3, x - 1),
        jnp.where(x == 0, 2, jnp.where(x == 3, 1, 0)),
        (x + 1) % ROW,
        x,
    )

    def step(k):
        j = turns[k]
        done = ROW - 1
        for earlier in turns[:k]:
            done = jnp.minimum(done, earlier)
        for slot in (2, 1, 0):

            @pl.when((z > 0) & (slot >= j) & (slot < done))
            def _():
                for t in (0, 1):
                    halo_wait(t, slot)

        if k < ROW - 1:
            d = (x + ROW - j) % ROW
            x_wait(2, d)
        attend(j)
        if k < ROW - 1:
            o_copy(j).start()
        else:
            o_local(j).start()

    step(0)

    step(1)

    step(2)

    for d in range(1, ROW):
        for m in range(5):

            @pl.when(l_used(m, x))
            def _():
                l_copy(m, d, (x + ROW - d) % ROW).wait_recv()

    def across(h, acc):
        hc = cols(h)
        squares = []
        states = lrecv[h].reshape(5 * hd, hd)
        for i in range(chunks):
            rows = pl.ds(i * chunk, chunk)
            far = jnp.dot(reached[h, rows, :], states, preferred_element_type=F32)
            out = (mixed[h, rows, :] + far) * gated[rows, hc]
            gated[rows, hc] = out
            squares.append(out * out)
        return tuple(a + s for a, s in zip(acc, squares))

    acc = lax.fori_loop(
        0, ROW, across, tuple(jnp.zeros((chunk, hd), F32) for _ in range(chunks))
    )
    nsend[...] = jnp.zeros_like(nsend)
    for i in range(chunks):
        nsend[i : i + 1, :] = jnp.sum(acc[i].T, axis=0, keepdims=True)
    for d in range(1, hn):
        n_copy(d).start()

    step(3)

    def mix_out(i):
        rows = pl.ds(i * chunk, chunk)
        return pltpu.make_async_copy(mout.at[rows], mo_hbm.at[rows], mix_sem.at[i])

    total = nsend[...]
    for d in range(1, hn):
        n_copy(d).wait_recv()
        total = total + nrecv[d - 1]
    gain_in.wait()
    scale = lax.rsqrt(total / (hn * ROW * hd) + 1e-05)
    for i in range(chunks):
        rows = pl.ds(i * chunk, chunk)
        scale_col = jnp.broadcast_to(scale[i : i + 1], (chunk, chunk)).T
        for h in range(ROW):
            hs = slice(h * hd, (h + 1) * hd)
            mout[rows, hs] = (gated[rows, hs] * scale_col * gainbuf[:, hs]).astype(BF16)
        mix_out(i).start()

    for d in range(1, ROW):
        for t in range(3):
            x_copy(t, d).wait_send()
        for c in s_copies(d):
            c.wait_send()
        for m in range(5):

            @pl.when(l_used(m, (x + d) % ROW))
            def _():
                l_copy(m, d, x).wait_send()

        @pl.when(relay_if(d))
        def _():
            for t in (0, 1):
                halo_relay(t, d).wait_send()

    @pl.when(own_halo)
    def _():
        for t in (0, 1):
            halo_own(t).wait_send()

    for d in group:

        @pl.when(zl + d < 4)
        def _():
            for c in r_copies(d):
                c.wait_send()

    for d in reaches:

        @pl.when((z == 3) & sends_to(d))
        def _():
            a_copy(d).wait_send()

    for d in range(1, hn):
        n_copy(d).wait_send()
    for j in range(ROW):

        @pl.when(x != j)
        def _():
            o_copy(j).wait_send()
            pltpu.make_async_remote_copy(
                src_ref=obuf.at[j],
                dst_ref=ao_hbm.at[:, cols(j)],
                send_sem=o_send.at[j],
                recv_sem=o_recv.at[j],
                device_id={"ctx": z * ROW + j},
                device_id_type=MESH,
            ).wait_recv()

        @pl.when(x == j)
        def _():
            o_local(j).wait()

    for i in range(chunks):
        mix_out(i).wait()


def hbm(*arrays):
    return [pltpu.with_memory_space_constraint(a, pltpu.HBM) for a in arrays]


def shards(zn, hn, sq, sk, sv, sg, ld, lg, gain, aq, ak, av):
    tok = sq.shape[0]
    heads = ld.shape[0]
    hd = sq.shape[1] // heads
    wide = heads * hd
    dma = pltpu.SemaphoreType.DMA
    vm = pltpu.VMEM
    anywhere = pl.BlockSpec(memory_space=pltpu.HBM)
    out = jax.ShapeDtypeStruct((tok, wide), BF16)
    return pl.pallas_call(
        functools.partial(kernel, zn, hn),
        out_shape=(out, out),
        in_specs=[anywhere] * 10,
        out_specs=(anywhere, anywhere),
        scratch_shapes=[
            vm((tok, wide), BF16),
            vm((tok, wide), BF16),
            vm((tok, wide), BF16),
            vm((tok, wide), BF16),
            vm((4, tok, hd), BF16),
            vm((7, tok, hd), BF16),
            vm((7, tok, hd), BF16),
            vm((4, tok, hd), BF16),
            vm((lg.shape[1], heads, tok), F32),
            vm((heads, tok), F32),
            vm((1, wide), F32),
            vm((heads, 32, tok), F32),
            vm((heads, tok, 32), F32),
            vm((heads, tok, hd), F32),
            vm((tok, wide), F32),
            vm((heads, tok, 5 * hd), BF16),
            vm((tok, wide), BF16),
            vm((4, hd, hd), BF16),
            vm((4, hd, hd), BF16),
            vm((4, 8, 128), F32),
            vm((4, 8, 128), F32),
            vm((hd, hd), BF16),
            vm((3, hd, hd), BF16),
            vm((8, 128), F32),
            vm((3, 8, 128), F32),
            vm((hd, hd), BF16),
            vm((hd, hd), BF16),
            vm((4, 5, hd, hd), BF16),
            vm((4, 5, hd, hd), BF16),
            vm((8, 128), F32),
            vm((max(hn - 1, 1), 8, 128), F32),
            dma((10,)),
            dma((3, 3)),
            dma((3, 3)),
            dma((2, 4)),
            dma((2, 4)),
            dma((2, 3)),
            dma((2, 3)),
            dma((2, 3)),
            dma((2, 3)),
            dma((5, 3)),
            dma((5, 3)),
            dma((max(hn - 1, 1),)),
            dma((max(hn - 1, 1),)),
            dma((4,)),
            dma((4,)),
            dma((2,)),
            dma((4,)),
            pltpu.SemaphoreType.REGULAR((4,)),
            dma((4,)),
            dma((1,)),
        ],
        compiler_params=pltpu.CompilerParams(
            collective_id=0, has_side_effects=True, vmem_limit_bytes=48 * 1024 * 1024
        ),
        cost_estimate=pl.CostEstimate(
            flops=3_000_000_000, bytes_accessed=5_000_000, transcendentals=5_000_000
        ),
    )(*hbm(sq, sk, sv, sg, ld, jnp.transpose(lg, (1, 0, 2)), gain.reshape(1, wide), aq, ak, av))


def solution(mesh):
    zn = mesh.shape["ctx"] // ROW
    hn = mesh.shape["head"]
    return jax.shard_map(
        functools.partial(shards, zn, hn),
        mesh=mesh,
        in_specs=(
            P("ctx", "head"),
            P("ctx", "head"),
            P("ctx", "head"),
            P("ctx", "head"),
            P("head", "ctx"),
            P("head", None, "ctx"),
            P("head"),
            P("ctx", "head"),
            P("ctx", "head"),
            P("ctx", "head"),
        ),
        out_specs=(P("ctx", "head"), P("ctx", "head")),
        check_vma=False,
    )
```
